32 devices in a mesh: chan: 4 (over z), blk: 8 (over y, x, core).
Axes of the slice: x: 2, y: 2, z: 4, core: 2. Of those that a mesh axis runs over, the one named last changes fastest.
Arguments:
- sky_maps: bfloat16 [256, 128, 2048], P('chan', 'blk'), may hold values from -6 to 6
- filters: bfloat16 [1024, 256, 256], P(('chan', 'blk')), may hold values from -0.375 to 0.375
- band_order_values: int32 [128], replicated, may hold values from 0 to 1023, as said below
- slot_degree_values: int32 [1024], replicated, may hold values from 0 to 1023, as said below
Outputs:
- cleaned_maps: bfloat16 [256, 128, 2048], P('chan', 'blk')
The draws below stay inside these ranges and needn't reach their ends.
Inputs may be any that keep to these rules, and one draw needn't show every extreme that they name: `band_order_values`: distinct orders; 0 and 1023 both occur. `slot_degree_values`: a permutation of the degrees; slots 2 i and 2 i + 1 hold degrees that sum to 1023.
All inputs are finite; a program needn't handle non-finite values.
Results may differ from the reference program's by a relative error of at most 0.015.
Values may be sent and summed in bfloat16 or wider, within the bound.
No kernel may reach another device: no remote copies, remote signals or barrier semaphores. Data moves between devices by JAX's collectives and lax.ppermute only.
A program may use at most 128 MiB of HBM per device.

```python
import math
import jax
import jax.numpy as jnp
from jax import lax

C = 256
LMAX = 1023
NPHI = 2048
M_DEV = 16
L = 1024
MW = 128
CYCLES = 128


def draw_band_order_values(key, part):
    inner = jax.random.permutation(jax.random.fold_in(key, 11), LMAX - 1)[:MW - 2].astype(jnp.int32) + 1
    chosen = jnp.concatenate([jnp.array([0, LMAX], jnp.int32), inner])
    reorder_slots = jax.random.permutation(jax.random.fold_in(key, 12), MW).astype(jnp.int32)
    return chosen[reorder_slots]


def draw_slot_degree_values(key, part):
    half_count = L // 2
    paired = jax.random.permutation(jax.random.fold_in(key, 21), half_count).astype(jnp.int32)
    flipped = jax.random.randint(jax.random.fold_in(key, 22), (half_count,), 0, 2).astype(jnp.int32)
    lower = paired + flipped * (L - 1 - 2 * paired)
    upper = L - 1 - lower
    return jnp.stack([lower, upper], axis=1).reshape(L)


def shard_levels(stream_key, dims, split, least, high):
    gain = 1.0
    for dim, shards_of in split:
        heights = jax.random.uniform(jax.random.fold_in(jax.random.fold_in(stream_key, 6), dim), (shards_of,), jnp.float32, least / len(split), high / len(split))
        gain = gain * jnp.repeat(jnp.exp(heights), dims[dim] // shards_of).reshape((-1,) + (1,) * (len(dims) - 1 - dim))
    return gain


def normal_values(own_key, shape, deviation, limit, split=(), kind=jnp.bfloat16):
    factor_of = shard_levels(own_key, shape, split, -0.22, 0.18) if split else 1.0
    values = jax.random.normal(own_key, shape, jnp.float32) * deviation * factor_of
    return jnp.minimum(jnp.maximum(values, -limit), limit).astype(kind)


def setup_inputs(seed: int = 0) -> dict:
    key_of = jax.random.split(jax.random.key(seed), 5)
    sky_maps = normal_values(key_of[0], (C, CYCLES, NPHI), 1.0, 6.0, ((0, 4), (1, 8)))
    filters = normal_values(key_of[1], (L, C, C), C ** -0.5, 0.375, ((0, 32),))
    band_order_values = draw_band_order_values(jax.random.fold_in(key_of[4], 71), 0)
    slot_degree_values = draw_slot_degree_values(jax.random.fold_in(key_of[4], 71), 0)
    return dict(sky_maps=sky_maps, filters=filters, band_order_values=band_order_values, slot_degree_values=slot_degree_values)


BAND = 0.38

def polar_angle_values(cycle_total):
    position = (jnp.arange(cycle_total, dtype=jnp.float32) + 0.5) / cycle_total
    return 0.5 * math.pi + BAND * (2.0 * position - 1.0)

def phase_table(mode_ids, pixel_count):
    pixels = jnp.arange(pixel_count, dtype=jnp.int32)
    rotations = pixels[:, None] * mode_ids[None, :] % pixel_count
    angles = 2.0 * math.pi / pixel_count * rotations.astype(jnp.float32)
    return jnp.stack([jnp.cos(angles), -jnp.sin(angles)], axis=-1)

def legendre(colatitude, mode_ids, levels):
    cosine = jnp.cos(colatitude)[:, None]
    sine_col = jnp.sin(colatitude)[:, None]
    orders = mode_ids.astype(jnp.float32)[None, :]
    log_seed = 0.5 * (jnp.log(orders + 0.5) + lax.lgamma(orders + 0.5) - lax.lgamma(orders + 1.0) - 0.5 * math.log(math.pi))
    seeded = jnp.exp(log_seed + orders * jnp.log(sine_col))

    def advance(carry, degree):
        latest, earlier = carry
        level = degree.astype(jnp.float32)
        growth = jnp.sqrt(jnp.maximum(4.0 * level * level - 1.0, 1.0) / jnp.maximum(level * level - orders * orders, 1.0))
        previous = level - 1.0
        shrink = jnp.sqrt(jnp.maximum(4.0 * previous * previous - 1.0, 1.0) / jnp.maximum(previous * previous - orders * orders, 1.0))
        upward = growth * (cosine * latest - earlier / shrink)
        current = jnp.where(level < orders, 0.0, jnp.where(level == orders, seeded, upward))
        return ((current, latest), current.astype(jnp.bfloat16))
    zeroed = jnp.zeros(seeded.shape, jnp.float32)
    degrees = jnp.arange(levels, dtype=jnp.int32)
    return lax.scan(advance, (zeroed, zeroed), degrees, unroll=8)[1]

def reference(sky_maps, filters, band_order_values, slot_degree_values):
    channels, cycle_total, pixel_count = sky_maps.shape
    degree_count = slot_degree_values.shape[0]
    mode_count = band_order_values.shape[0]
    colatitude = polar_angle_values(cycle_total)
    phases = phase_table(band_order_values, pixel_count).astype(jnp.bfloat16)
    product = jnp.dot(sky_maps.reshape(channels * cycle_total, pixel_count), phases.reshape(pixel_count, 2 * mode_count), preferred_element_type=jnp.float32)
    cycle_factor = 2.0 * math.sqrt(2.0 * BAND / cycle_total) * jnp.sin(colatitude) * (1.0 / math.sqrt(pixel_count))
    spectra = (product.reshape(channels, cycle_total, mode_count, 2) * cycle_factor[None, :, None, None]).astype(jnp.bfloat16)
    inverse = jnp.zeros((degree_count,), jnp.int32).at[slot_degree_values].set(jnp.arange(degree_count, dtype=jnp.int32))
    by_degree = filters[inverse].astype(jnp.float32)
    groups = mode_count // M_DEV
    mode_groups = band_order_values.reshape(groups, M_DEV)
    spec_groups = spectra.reshape(channels, cycle_total, groups, M_DEV, 2).transpose(2, 0, 1, 3, 4)

    def one_group(pair):
        mode_ids, spec_part = pair
        lat = legendre(colatitude, mode_ids, degree_count).astype(jnp.float32)
        coeffs = jnp.einsum('lrm,crmk->lcmk', lat, spec_part.astype(jnp.float32), precision=lax.Precision.HIGHEST).astype(jnp.bfloat16)
        filtered = jnp.einsum('loc,lcmk->lomk', by_degree, coeffs.astype(jnp.float32), precision=lax.Precision.HIGHEST).astype(jnp.bfloat16)
        cycle_part = 2.0 / math.sqrt(degree_count) * jnp.einsum('lrm,lomk->ormk', lat, filtered.astype(jnp.float32), precision=lax.Precision.HIGHEST)
        return cycle_part.astype(jnp.bfloat16)
    parts = lax.map(one_group, (mode_groups, spec_groups))
    cycle_all = parts.transpose(1, 2, 0, 3, 4).reshape(channels * cycle_total, 2 * mode_count)
    cleaned = jnp.dot(cycle_all, phases.reshape(pixel_count, 2 * mode_count).T, preferred_element_type=jnp.float32)
    return (cleaned * (1.0 / math.sqrt(mode_count))).astype(jnp.bfloat16).reshape(channels, cycle_total, pixel_count)
```

```python
import functools
import math

import jax
import jax.numpy as jnp
from jax import lax
from jax.experimental import pallas as pl
from jax.experimental.pallas import tpu as pltpu
from jax.sharding import PartitionSpec as P

BAND = 0.38
VMEM_LIMIT = 56 * 1024 * 1024
F32 = jnp.float32
BF16 = jnp.bfloat16


def params(**kw):
    return pltpu.CompilerParams(vmem_limit_bytes=VMEM_LIMIT, **kw)


def polar_angle_values(cycle_total):
    position = (jnp.arange(cycle_total, dtype=F32) + 0.5) / cycle_total
    return 0.5 * math.pi + BAND * (2.0 * position - 1.0)


def divisor(n, most):
    return max(d for d in range(1, most + 1) if n % d == 0)


def lane_blocks(width):
    return -(-width // 128)


def put(ref, rows, value):
    width = value.shape[1]
    for h in range(ref.shape[0]):
        piece = value[:, h * 128 : min((h + 1) * 128, width)]
        if piece.shape[1] < 128:
            piece = jnp.concatenate([piece, jnp.zeros((piece.shape[0], 128 - piece.shape[1]), piece.dtype)], axis=1)
        ref[h, rows, :] = piece


def get(ref, rows, width):
    value = jnp.concatenate([ref[h, rows, :] for h in range(ref.shape[0])], axis=1)
    return value if width == value.shape[1] else value[:, :width]


def analysis_kernel(steps, factor_ref, modes_ref, sky_ref, out_ref, phase_ref, prod_ref, turn_ref):
    step = pl.program_id(0)
    chans, cycles, pixels = sky_ref.shape
    modes = modes_ref.shape[1]
    low = 64
    high = pixels // low

    @pl.when(step == 0)
    def _():
        ids = modes_ref[...]
        unit = 2.0 * math.pi / pixels

        def table(rows, stride):
            index = lax.broadcasted_iota(jnp.int32, (rows, modes), 0) * stride
            angle = unit * ((index * ids) & (pixels - 1)).astype(F32)
            return jnp.cos(angle), jnp.sin(angle)

        cos_low, sin_low = table(low, 1)
        cos_high, sin_high = table(high, low)
        for h in range(high):
            ca, sa = cos_high[h : h + 1], sin_high[h : h + 1]
            rows = slice(h * low, (h + 1) * low)
            phase_ref[rows, :modes] = (ca * cos_low - sa * sin_low).astype(BF16)
            phase_ref[rows, modes:] = (-(sa * cos_low + ca * sin_low)).astype(BF16)

    rows = chans * cycles
    product = jnp.dot(sky_ref[...].reshape(rows, pixels), phase_ref[...], preferred_element_type=F32)
    put(prod_ref, pl.ds(pl.multiple_of(step * rows, rows), rows), product)

    @pl.when(step == steps - 1)
    def _():
        total = chans * steps
        for r in range(cycles):
            part = get(prod_ref, pl.ds(r, total, stride=cycles), 2 * modes) * factor_ref[r]
            both = [part[:, k * modes : (k + 1) * modes].T for k in range(2)]
            put(turn_ref, pl.ds(r, modes, stride=cycles), jnp.concatenate(both, axis=1))
        out_ref[...] = get(turn_ref, slice(None), 2 * total).astype(BF16).reshape(out_ref.shape)


def analysis(sky, factor, modes):
    chans, cycles, pixels = sky.shape
    count = modes.shape[0]
    steps = 4
    return pl.pallas_call(
        functools.partial(analysis_kernel, steps),
        grid=(steps,),
        in_specs=[
            pl.BlockSpec(memory_space=pltpu.SMEM),
            pl.BlockSpec((1, count), lambda i: (0, 0)),
            pl.BlockSpec((chans // steps, cycles, pixels), lambda i: (i, 0, 0)),
        ],
        out_specs=pl.BlockSpec((count, cycles, 2 * chans), lambda i: (0, 0, 0)),
        out_shape=jax.ShapeDtypeStruct((count, cycles, 2 * chans), BF16),
        scratch_shapes=[
            pltpu.VMEM((pixels, 2 * count), BF16),
            pltpu.VMEM((lane_blocks(2 * count), chans * cycles, 128), F32),
            pltpu.VMEM((lane_blocks(2 * chans), count * cycles, 128), F32),
        ],
        compiler_params=params(),
        name="analysis",
    )(factor, modes.reshape(1, count), sky)


def legendre_kernel(levels, degree_ref, order_ref, cosine_ref, seed_ref, lat_ref, turned_ref, gain_ref, all_ref, pick_ref):
    modes, cycles = seed_ref.shape
    slots = lat_ref.shape[1]
    block = 128
    level = lax.broadcasted_iota(jnp.int32, (modes, levels), 1).astype(F32)
    squared = order_ref[...] * order_ref[...]

    def growth(n):
        return jnp.sqrt(jnp.maximum(4.0 * n * n - 1.0, 1.0) / jnp.maximum(n * n - squared, 1.0))

    here = growth(level)
    gain_ref[0] = here
    gain_ref[1] = here / growth(level - 1.0)
    cosine = jnp.broadcast_to(cosine_ref[...], (modes, cycles))
    orders = jnp.broadcast_to(order_ref[...], (modes, cycles))
    seed = seed_ref[...]

    def advance(i, carry):
        latest, earlier = carry
        start = pl.multiple_of(i * block, block)
        first = gain_ref[0, :, pl.ds(start, block)]
        second = gain_ref[1, :, pl.ds(start, block)]
        base = (i * block).astype(F32)
        for n in range(block):
            up = jnp.broadcast_to(first[:, n : n + 1], (modes, cycles)) * cosine
            down = jnp.broadcast_to(second[:, n : n + 1], (modes, cycles))
            begin = jnp.where(orders == base + n, seed, 0.0)
            current = up * latest + (begin - down * earlier)
            put(all_ref, pl.ds(pl.multiple_of((start + n) * modes, modes), modes), current)
            latest, earlier = current, latest
        return latest, earlier

    zero = jnp.zeros((modes, cycles), F32)
    lax.fori_loop(0, levels // block, advance, (zero, zero))

    def pick(s, _):
        source = pl.multiple_of(degree_ref[s] * modes, modes)
        for h in range(all_ref.shape[0]):
            pick_ref[h, pl.ds(pl.multiple_of(s * modes, modes), modes), :] = all_ref[h, pl.ds(source, modes), :]
        return 0

    lax.fori_loop(0, slots, pick, 0, unroll=8)
    for j in range(modes):
        rows = get(pick_ref, pl.ds(j, slots, stride=modes), cycles)
        lat_ref[j] = rows.astype(BF16)
        turned_ref[j] = rows.T.astype(BF16)


def legendre(degrees, orders, colatitude, levels):
    slots, modes, cycles = degrees.shape[0], orders.shape[0], colatitude.shape[0]
    m = orders.astype(F32)[:, None]
    log_seed = 0.5 * (
        jnp.log(m + 0.5) + lax.lgamma(m + 0.5) - lax.lgamma(m + 1.0) - 0.5 * math.log(math.pi)
    )
    seed = jnp.exp(log_seed + m * jnp.log(jnp.sin(colatitude))[None, :])
    vmem = pl.BlockSpec(memory_space=pltpu.VMEM)
    return pl.pallas_call(
        functools.partial(legendre_kernel, levels),
        in_specs=[pl.BlockSpec(memory_space=pltpu.SMEM), vmem, vmem, vmem],
        out_specs=[vmem, vmem],
        out_shape=[
            jax.ShapeDtypeStruct((modes, slots, cycles), BF16),
            jax.ShapeDtypeStruct((modes, cycles, slots), BF16),
        ],
        scratch_shapes=[
            pltpu.VMEM((2, modes, levels), F32),
            pltpu.VMEM((lane_blocks(cycles), levels * modes, 128), F32),
            pltpu.VMEM((lane_blocks(cycles), slots * modes, 128), F32),
        ],
        compiler_params=params(),
        cost_estimate=pl.CostEstimate(flops=40_000_000, bytes_accessed=4_000_000, transcendentals=0),
        name="legendre",
    )(degrees, m, jnp.cos(colatitude)[None, :], seed)


def harmonic_kernel(place_ref, lat_ref, *refs):
    parts = len(refs) - 4
    spectra, out_ref, all_ref, wide_ref, turn_ref = refs[:parts], *refs[parts:]
    groups, modes, cycles, pair = spectra[0].shape
    chans = pair // 2
    total = chans * parts
    dests, slot_dev = out_ref.shape[:2]
    slots = dests * slot_dev
    rows = 2 * modes
    step = pl.program_id(0)

    @pl.when(step == 0)
    def _():
        for t in range(parts):
            all_ref[place_ref[t]] = spectra[t][...]
        for j in range(modes):
            pieces = [all_ref[z, :, j].reshape(groups * cycles, pair) for z in range(parts)]
            for k in range(2):
                wide_ref[j, :, k * total : (k + 1) * total] = jnp.concatenate(
                    [p[:, k * chans : (k + 1) * chans] for p in pieces], axis=1
                )

    lanes = turn_ref.shape[2]
    for j in range(modes):
        result = jnp.dot(lat_ref[j], wide_ref[j], preferred_element_type=F32)
        for k in range(2):
            for h in range(total // lanes):
                turn_ref[h, pl.ds(2 * j + k, slots, stride=rows), :] = result[
                    :, k * total + h * lanes : k * total + (h + 1) * lanes
                ]
    for h in range(total // lanes):
        out_ref[:, :, :, h * lanes : (h + 1) * lanes] = (
            turn_ref[h].astype(BF16).reshape(dests, slot_dev, rows, lanes)
        )


def harmonic(place, lat, spectra, slot_dev):
    modes, slots, cycle_total = lat.shape
    groups, _, cycles, pair = spectra[0].shape
    total = pair // 2 * len(spectra)
    dests = slots // slot_dev
    steps = divisor(dests, 2)
    lanes = min(128, total)
    whole = pl.BlockSpec((groups, modes, cycles, pair), lambda i: (0, 0, 0, 0))
    return pl.pallas_call(
        harmonic_kernel,
        grid=(steps,),
        in_specs=[
            pl.BlockSpec(memory_space=pltpu.SMEM),
            pl.BlockSpec((modes, slots // steps, cycle_total), lambda i: (0, i, 0)),
        ]
        + [whole] * len(spectra),
        out_specs=pl.BlockSpec((dests // steps, slot_dev, 2 * modes, total), lambda i: (i, 0, 0, 0)),
        out_shape=jax.ShapeDtypeStruct((dests, slot_dev, 2 * modes, total), BF16),
        scratch_shapes=[
            pltpu.VMEM((len(spectra), groups, modes, cycles, pair), BF16),
            pltpu.VMEM((modes, cycle_total, 2 * total), BF16),
            pltpu.VMEM((total // lanes, slots // steps * 2 * modes, lanes), F32),
        ],
        compiler_params=params(),
        name="harmonic",
    )(place, lat, *spectra)


def filter_kernel(filters_ref, coeffs_ref, out_ref, turn_ref):
    groups, slots, rows, total = coeffs_ref.shape
    lanes = turn_ref.shape[2]
    for s in range(slots):
        result = lax.dot_general(
            coeffs_ref[:, s].reshape(groups * rows, total),
            filters_ref[s],
            (((1,), (1,)), ((), ())),
            preferred_element_type=F32,
        )
        for h in range(total // lanes):
            turn_ref[h, pl.ds(s, groups * rows, stride=slots), :] = result[:, h * lanes : (h + 1) * lanes]
    for h in range(total // lanes):
        out_ref[:, :, :, h * lanes : (h + 1) * lanes] = (
            turn_ref[h].astype(BF16).reshape(groups, rows, slots, lanes)
        )


def apply_filters(filters, coeffs):
    groups, slots, rows, total = coeffs.shape
    step = min(slots, 16)
    lanes = min(128, total)
    return pl.pallas_call(
        filter_kernel,
        grid=(slots // step,),
        in_specs=[
            pl.BlockSpec((step, total, total), lambda i: (i, 0, 0)),
            pl.BlockSpec((groups, step, rows, total), lambda i: (0, i, 0, 0)),
        ],
        out_specs=pl.BlockSpec((groups, rows, step, total), lambda i: (0, 0, i, 0)),
        out_shape=jax.ShapeDtypeStruct((groups, rows, slots, total), BF16),
        scratch_shapes=[pltpu.VMEM((total // lanes, groups * rows * step, lanes), F32)],
        compiler_params=params(),
        name="filters",
    )(filters, coeffs)


def cycles_kernel(scale, place_ref, turned_ref, filtered_ref, out_ref):
    groups, rows, slot_dev, total = filtered_ref.shape
    parts, blocks, modes, cycles, pair = out_ref.shape
    chans = pair // 2
    for j in range(modes):
        result = [
            jnp.dot(
                turned_ref[j],
                filtered_ref[:, 2 * j + k].reshape(groups * slot_dev, total),
                preferred_element_type=F32,
            )
            for k in range(2)
        ]
        for z in range(parts):
            piece = jnp.concatenate([r[:, z * chans : (z + 1) * chans] for r in result], axis=1) * scale
            out_ref[place_ref[z], :, j] = piece.astype(BF16).reshape(blocks, cycles, pair)


def to_cycles(place, turned, filtered, scale, blocks, parts):
    modes, cycle_total, slots = turned.shape
    groups, rows, slot_dev, total = filtered.shape
    vmem = pl.BlockSpec(memory_space=pltpu.VMEM)
    return pl.pallas_call(
        functools.partial(cycles_kernel, scale),
        in_specs=[pl.BlockSpec(memory_space=pltpu.SMEM), vmem, vmem],
        out_specs=vmem,
        out_shape=jax.ShapeDtypeStruct(
            (parts, blocks, modes, cycle_total // blocks, 2 * total // parts), BF16
        ),
        compiler_params=params(),
        name="cycles",
    )(place, turned, filtered)


def synthesis_kernel(modes_ref, parts_ref, out_ref, phase_ref, wide_ref, turn_ref, left_ref):
    step = pl.program_id(0)
    chans, cycles, pixels = out_ref.shape
    modes, _, pair = parts_ref.shape
    low = 128
    total = pair // 2

    @pl.when(step == 0)
    def _():
        ids = modes_ref[...]
        unit = 2.0 * math.pi / pixels

        def table(columns, stride):
            index = lax.broadcasted_iota(jnp.int32, (modes, columns), 1) * stride
            angle = unit * ((index * ids) & (pixels - 1)).astype(F32)
            return jnp.cos(angle), jnp.sin(angle)

        cos_low, sin_low = table(low, 1)
        cos_high, sin_high = table(pixels // low, low)
        for h in range(pixels // low):
            ca, sa = cos_high[:, h : h + 1], sin_high[:, h : h + 1]
            columns = slice(h * low, (h + 1) * low)
            phase_ref[:modes, columns] = (ca * cos_low - sa * sin_low).astype(BF16)
            phase_ref[modes:, columns] = (-(sa * cos_low + ca * sin_low)).astype(BF16)
        put(wide_ref, slice(None), parts_ref[...].astype(F32).reshape(modes * cycles, pair))
        for r in range(cycles):
            part = get(wide_ref, pl.ds(r, modes, stride=cycles), pair)
            both = [part[:, k * total : (k + 1) * total].T for k in range(2)]
            put(turn_ref, pl.ds(r, total, stride=cycles), jnp.concatenate(both, axis=1))
        left_ref[...] = get(turn_ref, slice(None), 2 * modes).astype(BF16)

    rows = chans * cycles
    result = jnp.dot(
        left_ref[pl.ds(pl.multiple_of(step * rows, rows), rows), :], phase_ref[...], preferred_element_type=F32
    )
    out_ref[...] = (result * (1.0 / math.sqrt(modes))).astype(BF16).reshape(chans, cycles, pixels)


def synthesis(parts, modes, pixels):
    count, cycles, pair = parts.shape
    chans = pair // 2
    steps = 4
    return pl.pallas_call(
        synthesis_kernel,
        grid=(steps,),
        in_specs=[
            pl.BlockSpec((count, 1), lambda i: (0, 0)),
            pl.BlockSpec((count, cycles, pair), lambda i: (0, 0, 0)),
        ],
        out_specs=pl.BlockSpec((chans // steps, cycles, pixels), lambda i: (i, 0, 0)),
        out_shape=jax.ShapeDtypeStruct((chans, cycles, pixels), BF16),
        scratch_shapes=[
            pltpu.VMEM((2 * count, pixels), BF16),
            pltpu.VMEM((lane_blocks(pair), count * cycles, 128), F32),
            pltpu.VMEM((lane_blocks(2 * count), chans * cycles, 128), F32),
            pltpu.VMEM((chans * cycles, 2 * count), BF16),
        ],
        compiler_params=params(),
        name="synthesis",
    )(modes.reshape(count, 1), parts)


def body(sky_maps, filters, band_order_values, slot_degree_values):
    chans, cycle_dev, pixels = sky_maps.shape
    chan_groups = lax.axis_size("chan")
    blk_groups = lax.axis_size("blk")
    chan, blk = lax.axis_index("chan"), lax.axis_index("blk")
    slot_dev = filters.shape[0]
    degree_count = slot_degree_values.shape[0]
    mode_dev = band_order_values.shape[0] // blk_groups
    cycle_total = cycle_dev * blk_groups
    group_slots = slot_dev * blk_groups
    colatitude = polar_angle_values(cycle_total)
    cycle_factor = (
        2.0 * math.sqrt(2.0 * BAND / cycle_total) * jnp.sin(colatitude) * (1.0 / math.sqrt(pixels))
    )
    local_factor = lax.dynamic_slice_in_dim(cycle_factor, blk * cycle_dev, cycle_dev)
    local_modes = lax.dynamic_slice_in_dim(band_order_values, blk * mode_dev, mode_dev)
    degrees = lax.dynamic_slice_in_dim(slot_degree_values, chan * group_slots, group_slots)

    spectra = analysis(sky_maps, local_factor, band_order_values)
    spectra = spectra.reshape(blk_groups, mode_dev, cycle_dev, 2 * chans)
    spectra = lax.all_to_all(spectra, "blk", split_axis=0, concat_axis=0, tiled=True)
    shift = [[(i, (i + t) % chan_groups) for i in range(chan_groups)] for t in range(chan_groups)]
    gathered = [spectra] + [lax.ppermute(spectra, "chan", shift[t]) for t in range(1, chan_groups)]
    lat, turned = legendre(degrees, local_modes, colatitude, degree_count)
    hops = jnp.arange(chan_groups, dtype=jnp.int32)
    coeffs = harmonic((chan - hops) % chan_groups, lat, gathered, slot_dev)
    coeffs = lax.all_to_all(coeffs, "blk", split_axis=0, concat_axis=0, tiled=True)
    filtered = apply_filters(filters, coeffs)
    filtered = lax.all_to_all(filtered, "blk", split_axis=0, concat_axis=0, tiled=True)
    scale = 2.0 / math.sqrt(degree_count)
    partial = to_cycles((hops - chan) % chan_groups, turned, filtered, scale, blk_groups, chan_groups)
    arrived = [partial[0]] + [lax.ppermute(partial[t], "chan", shift[t]) for t in range(1, chan_groups)]
    cycle_part = functools.reduce(jnp.add, [a.astype(F32) for a in arrived]).astype(BF16)
    by_cycle = lax.all_to_all(cycle_part, "blk", split_axis=0, concat_axis=0, tiled=True)
    by_cycle = by_cycle.reshape(blk_groups * mode_dev, cycle_dev, 2 * chans)
    return synthesis(by_cycle, band_order_values, pixels)


def solution(mesh):
    in_specs = (P("chan", "blk", None), P(("chan", "blk"), None, None), P(), P())
    out_specs = P("chan", "blk", None)
    return jax.shard_map(body, mesh=mesh, in_specs=in_specs, out_specs=out_specs, check_vma=False)
```

```python
import functools
import math

import jax
import jax.numpy as jnp
from jax import lax
from jax.experimental import pallas as pl
from jax.experimental.pallas import tpu as pltpu
from jax.sharding import PartitionSpec as P

BAND = 0.38
VMEM_LIMIT = 56 * 1024 * 1024
F32 = jnp.float32
BF16 = jnp.bfloat16
COST = pl.CostEstimate(flops=2_000_000_000, bytes_accessed=12_000_000, transcendentals=0)


def params(**kw):
    return pltpu.CompilerParams(vmem_limit_bytes=VMEM_LIMIT, **kw)


def polar_angle_values(cycle_total):
    position = (jnp.arange(cycle_total, dtype=F32) + 0.5) / cycle_total
    return 0.5 * math.pi + BAND * (2.0 * position - 1.0)


def divisor(n, most):
    return max(d for d in range(1, most + 1) if n % d == 0)


def lane_blocks(width):
    return -(-width // 128)


def put(ref, rows, value):
    width = value.shape[1]
    for h in range(ref.shape[0]):
        piece = value[:, h * 128 : min((h + 1) * 128, width)]
        if piece.shape[1] < 128:
            piece = jnp.concatenate([piece, jnp.zeros((piece.shape[0], 128 - piece.shape[1]), piece.dtype)], axis=1)
        ref[h, rows, :] = piece


def get(ref, rows, width):
    value = jnp.concatenate([ref[h, rows, :] for h in range(ref.shape[0])], axis=1)
    return value if width == value.shape[1] else value[:, :width]


def analysis_kernel(steps, factor_ref, modes_ref, sky_ref, out_ref, phase_ref, prod_ref, turn_ref):
    step = pl.program_id(0)
    chans, cycles, pixels = sky_ref.shape
    modes = modes_ref.shape[1]
    low = 64
    high = pixels // low

    @pl.when(step == 0)
    def _():
        ids = modes_ref[...]
        unit = 2.0 * math.pi / pixels

        def table(rows, stride):
            index = lax.broadcasted_iota(jnp.int32, (rows, modes), 0) * stride
            angle = unit * ((index * ids) & (pixels - 1)).astype(F32)
            return jnp.cos(angle), jnp.sin(angle)

        cos_low, sin_low = table(low, 1)
        cos_high, sin_high = table(high, low)
        for h in range(high):
            ca, sa = cos_high[h : h + 1], sin_high[h : h + 1]
            rows = slice(h * low, (h + 1) * low)
            phase_ref[rows, :modes] = (ca * cos_low - sa * sin_low).astype(BF16)
            phase_ref[rows, modes:] = (-(sa * cos_low + ca * sin_low)).astype(BF16)

    rows = chans * cycles
    product = jnp.dot(sky_ref[...].reshape(rows, pixels), phase_ref[...], preferred_element_type=F32)
    put(prod_ref, pl.ds(pl.multiple_of(step * rows, rows), rows), product)

    @pl.when(step == steps - 1)
    def _():
        total = chans * steps
        for r in range(cycles):
            part = get(prod_ref, pl.ds(r, total, stride=cycles), 2 * modes) * factor_ref[r]
            both = [part[:, k * modes : (k + 1) * modes].T for k in range(2)]
            put(turn_ref, pl.ds(r, modes, stride=cycles), jnp.concatenate(both, axis=1))
        out_ref[...] = get(turn_ref, slice(None), 2 * total).astype(BF16).reshape(out_ref.shape)


def analysis(sky, factor, modes):
    chans, cycles, pixels = sky.shape
    count = modes.shape[0]
    steps = 4
    return pl.pallas_call(
        functools.partial(analysis_kernel, steps),
        grid=(steps,),
        in_specs=[
            pl.BlockSpec(memory_space=pltpu.SMEM),
            pl.BlockSpec((1, count), lambda i: (0, 0)),
            pl.BlockSpec((chans // steps, cycles, pixels), lambda i: (i, 0, 0)),
        ],
        out_specs=pl.BlockSpec((count, cycles, 2 * chans), lambda i: (0, 0, 0)),
        out_shape=jax.ShapeDtypeStruct((count, cycles, 2 * chans), BF16),
        scratch_shapes=[
            pltpu.VMEM((pixels, 2 * count), BF16),
            pltpu.VMEM((lane_blocks(2 * count), chans * cycles, 128), F32),
            pltpu.VMEM((lane_blocks(2 * chans), count * cycles, 128), F32),
        ],
        compiler_params=params(),
        name="analysis",
    )(factor, modes.reshape(1, count), sky)


def legendre_kernel(levels, degree_ref, order_ref, cosine_ref, seed_ref, lat_ref, turned_ref, gain_ref, all_ref, pick_ref):
    modes, cycles = seed_ref.shape
    slots = lat_ref.shape[1]
    block = 128
    level = lax.broadcasted_iota(jnp.int32, (modes, levels), 1).astype(F32)
    squared = order_ref[...] * order_ref[...]

    def growth(n):
        return jnp.sqrt(jnp.maximum(4.0 * n * n - 1.0, 1.0) / jnp.maximum(n * n - squared, 1.0))

    here = growth(level)
    gain_ref[0] = here
    gain_ref[1] = here / growth(level - 1.0)
    cosine = jnp.broadcast_to(cosine_ref[...], (modes, cycles))
    orders = jnp.broadcast_to(order_ref[...], (modes, cycles))
    seed = seed_ref[...]

    def advance(i, carry):
        latest, earlier = carry
        start = pl.multiple_of(i * block, block)
        first = gain_ref[0, :, pl.ds(start, block)]
        second = gain_ref[1, :, pl.ds(start, block)]
        base = (i * block).astype(F32)
        for n in range(block):
            up = jnp.broadcast_to(first[:, n : n + 1], (modes, cycles)) * cosine
            down = jnp.broadcast_to(second[:, n : n + 1], (modes, cycles))
            begin = jnp.where(orders == base + n, seed, 0.0)
            current = up * latest + (begin - down * earlier)
            put(all_ref, pl.ds(pl.multiple_of((start + n) * modes, modes), modes), current)
            latest, earlier = current, latest
        return latest, earlier

    zero = jnp.zeros((modes, cycles), F32)
    lax.fori_loop(0, levels // block, advance, (zero, zero))

    def pick(s, _):
        source = pl.multiple_of(degree_ref[s] * modes, modes)
        for h in range(all_ref.shape[0]):
            pick_ref[h, pl.ds(pl.multiple_of(s * modes, modes), modes), :] = all_ref[h, pl.ds(source, modes), :]
        return 0

    lax.fori_loop(0, slots, pick, 0, unroll=8)
    for j in range(modes):
        rows = get(pick_ref, pl.ds(j, slots, stride=modes), cycles)
        lat_ref[j] = rows.astype(BF16)
        turned_ref[j] = rows.T.astype(BF16)


def legendre(degrees, orders, colatitude, levels):
    slots, modes, cycles = degrees.shape[0], orders.shape[0], colatitude.shape[0]
    m = orders.astype(F32)[:, None]
    log_seed = 0.5 * (
        jnp.log(m + 0.5) + lax.lgamma(m + 0.5) - lax.lgamma(m + 1.0) - 0.5 * math.log(math.pi)
    )
    seed = jnp.exp(log_seed + m * jnp.log(jnp.sin(colatitude))[None, :])
    vmem = pl.BlockSpec(memory_space=pltpu.VMEM)
    return pl.pallas_call(
        functools.partial(legendre_kernel, levels),
        in_specs=[pl.BlockSpec(memory_space=pltpu.SMEM), vmem, vmem, vmem],
        out_specs=[vmem, vmem],
        out_shape=[
            jax.ShapeDtypeStruct((modes, slots, cycles), BF16),
            jax.ShapeDtypeStruct((modes, cycles, slots), BF16),
        ],
        scratch_shapes=[
            pltpu.VMEM((2, modes, levels), F32),
            pltpu.VMEM((lane_blocks(cycles), levels * modes, 128), F32),
            pltpu.VMEM((lane_blocks(cycles), slots * modes, 128), F32),
        ],
        compiler_params=params(),
        cost_estimate=pl.CostEstimate(flops=40_000_000, bytes_accessed=30_000_000, transcendentals=0),
        name="legendre",
    )(degrees, m, jnp.cos(colatitude)[None, :], seed)


def harmonic_kernel(lat_ref, *refs):
    parts = len(refs) - 2
    spectra, out_ref, turn_ref = refs[:parts], *refs[parts:]
    groups, modes, cycles, pair = spectra[0].shape
    slots = out_ref.shape[0] * out_ref.shape[1]
    for j in range(modes):
        for t in range(parts):
            result = jnp.dot(
                lat_ref[j], spectra[t][:, j].reshape(groups * cycles, pair), preferred_element_type=F32
            )
            put(turn_ref.at[t], pl.ds(j, slots, stride=modes), result)
    for t in range(parts):
        value = get(turn_ref.at[t], slice(None), pair).astype(BF16)
        out_ref[:, :, :, t * pair : (t + 1) * pair] = value.reshape(out_ref.shape[:3] + (pair,))


def harmonic(lat, spectra, slot_dev):
    modes, slots, cycle_total = lat.shape
    groups, _, cycles, pair = spectra[0].shape
    parts = len(spectra)
    dests = slots // slot_dev
    steps = divisor(dests, 2)
    whole = pl.BlockSpec((groups, modes, cycles, pair), lambda i: (0, 0, 0, 0))
    return pl.pallas_call(
        harmonic_kernel,
        grid=(steps,),
        in_specs=[pl.BlockSpec((modes, slots // steps, cycle_total), lambda i: (0, i, 0))] + [whole] * parts,
        out_specs=pl.BlockSpec((dests // steps, slot_dev, modes, parts * pair), lambda i: (i, 0, 0, 0)),
        out_shape=jax.ShapeDtypeStruct((dests, slot_dev, modes, parts * pair), BF16),
        scratch_shapes=[pltpu.VMEM((parts, lane_blocks(pair), slots // steps * modes, 128), F32)],
        compiler_params=params(),
        cost_estimate=COST,
        name="harmonic",
    )(lat, *spectra)


def filter_kernel(hops, counts, place_ref, filters_ref, *refs):
    inputs, outs, all_ref, turn_ref = refs[: len(counts)], refs[len(counts) : -2], *refs[-2:]
    groups, slots, modes, _ = inputs[0].shape
    pair = all_ref.shape[4]
    chans = pair // 2
    parts = all_ref.shape[0]
    t = 0
    for ref, count in zip(inputs, counts):
        for i in range(count):
            all_ref[place_ref[t]] = ref[:, :, :, i * pair : (i + 1) * pair]
            t += 1
    rows = groups * modes
    for s in range(slots):
        pieces = [all_ref[z, :, s].reshape(rows, pair) for z in range(parts)]
        both = [
            jnp.concatenate([p[:, k * chans : (k + 1) * chans] for p in pieces], axis=1) for k in range(2)
        ]
        left = jnp.concatenate(both, axis=0)
        for i, hop in enumerate(hops):
            start = pl.multiple_of(place_ref[hop] * chans, chans)
            result = lax.dot_general(
                left, filters_ref[s, pl.ds(start, chans), :], (((1,), (1,)), ((), ())), preferred_element_type=F32
            )
            put(
                turn_ref.at[i],
                pl.ds(s, rows, stride=slots),
                jnp.concatenate([result[:rows], result[rows:]], axis=1),
            )
    i = 0
    for ref in outs:
        for n in range(ref.shape[3] // pair):
            value = get(turn_ref.at[i], slice(None), pair).astype(BF16)
            ref[:, :, :, n * pair : (n + 1) * pair] = value.reshape(ref.shape[:3] + (pair,))
            i += 1


def apply_filters(place, filters, coeffs, counts, wanted):
    groups, slots, modes, _ = coeffs[0].shape
    total = filters.shape[2]
    pair = coeffs[0].shape[3] // counts[0]
    step = min(slots, 16)
    hops = sum(wanted, [])
    return pl.pallas_call(
        functools.partial(filter_kernel, hops, counts),
        grid=(slots // step,),
        in_specs=[
            pl.BlockSpec(memory_space=pltpu.SMEM),
            pl.BlockSpec((step, total, total), lambda i: (i, 0, 0)),
        ]
        + [pl.BlockSpec((groups, step, modes, n * pair), lambda i: (0, i, 0, 0)) for n in counts],
        out_specs=[
            pl.BlockSpec((groups, modes, step, len(w) * pair), lambda i: (0, 0, i, 0)) for w in wanted
        ],
        out_shape=[jax.ShapeDtypeStruct((groups, modes, slots, len(w) * pair), BF16) for w in wanted],
        scratch_shapes=[
            pltpu.VMEM((sum(counts), groups, step, modes, pair), BF16),
            pltpu.VMEM((len(hops), lane_blocks(pair), groups * modes * step, 128), F32),
        ],
        compiler_params=params(),
        cost_estimate=COST,
        name="filters",
    )(place, filters, *coeffs)


def cycles_kernel(scale, turned_ref, filtered_ref, *outs):
    groups, modes, slot_dev, width = filtered_ref.shape
    blocks, _, cycles, pair = outs[0].shape
    for j in range(modes):
        result = jnp.dot(
            turned_ref[j],
            filtered_ref[:, j].reshape(groups * slot_dev, width),
            preferred_element_type=F32,
        )
        result = (result * scale).astype(BF16)
        for t, ref in enumerate(outs):
            ref[:, j] = result[:, t * pair : (t + 1) * pair].reshape(blocks, cycles, pair)


def to_cycles(turned, filtered, scale, blocks, parts):
    modes, cycle_total, slots = turned.shape
    width = filtered.shape[3]
    vmem = pl.BlockSpec(memory_space=pltpu.VMEM)
    shape = (blocks, modes, cycle_total // blocks, width // parts)
    return pl.pallas_call(
        functools.partial(cycles_kernel, scale),
        in_specs=[vmem, vmem],
        out_specs=[vmem] * parts,
        out_shape=[jax.ShapeDtypeStruct(shape, BF16)] * parts,
        compiler_params=params(),
        cost_estimate=COST,
        name="cycles",
    )(turned, filtered)


def synthesis_kernel(modes_ref, parts_ref, out_ref, phase_ref, wide_ref, turn_ref, left_ref):
    step = pl.program_id(0)
    chans, cycles, pixels = out_ref.shape
    modes, _, pair = parts_ref.shape
    low = 128
    total = pair // 2

    @pl.when(step == 0)
    def _():
        ids = modes_ref[...]
        unit = 2.0 * math.pi / pixels

        def table(columns, stride):
            index = lax.broadcasted_iota(jnp.int32, (modes, columns), 1) * stride
            angle = unit * ((index * ids) & (pixels - 1)).astype(F32)
            return jnp.cos(angle), jnp.sin(angle)

        cos_low, sin_low = table(low, 1)
        cos_high, sin_high = table(pixels // low, low)
        for h in range(pixels // low):
            ca, sa = cos_high[:, h : h + 1], sin_high[:, h : h + 1]
            columns = slice(h * low, (h + 1) * low)
            phase_ref[:modes, columns] = (ca * cos_low - sa * sin_low).astype(BF16)
            phase_ref[modes:, columns] = (-(sa * cos_low + ca * sin_low)).astype(BF16)
        put(wide_ref, slice(None), parts_ref[...].astype(F32).reshape(modes * cycles, pair))
        for r in range(cycles):
            part = get(wide_ref, pl.ds(r, modes, stride=cycles), pair)
            both = [part[:, k * total : (k + 1) * total].T for k in range(2)]
            put(turn_ref, pl.ds(r, total, stride=cycles), jnp.concatenate(both, axis=1))
        left_ref[...] = get(turn_ref, slice(None), 2 * modes).astype(BF16)

    rows = chans * cycles
    result = jnp.dot(
        left_ref[pl.ds(pl.multiple_of(step * rows, rows), rows), :], phase_ref[...], preferred_element_type=F32
    )
    out_ref[...] = (result * (1.0 / math.sqrt(modes))).astype(BF16).reshape(chans, cycles, pixels)


def synthesis(parts, modes, pixels):
    count, cycles, pair = parts.shape
    chans = pair // 2
    steps = 4
    return pl.pallas_call(
        synthesis_kernel,
        grid=(steps,),
        in_specs=[
            pl.BlockSpec((count, 1), lambda i: (0, 0)),
            pl.BlockSpec((count, cycles, pair), lambda i: (0, 0, 0)),
        ],
        out_specs=pl.BlockSpec((chans // steps, cycles, pixels), lambda i: (i, 0, 0)),
        out_shape=jax.ShapeDtypeStruct((chans, cycles, pixels), BF16),
        scratch_shapes=[
            pltpu.VMEM((2 * count, pixels), BF16),
            pltpu.VMEM((lane_blocks(pair), count * cycles, 128), F32),
            pltpu.VMEM((lane_blocks(2 * count), chans * cycles, 128), F32),
            pltpu.VMEM((chans * cycles, 2 * count), BF16),
        ],
        compiler_params=params(),
        name="synthesis",
    )(modes.reshape(count, 1), parts)


def body(sky_maps, filters, band_order_values, slot_degree_values):
    chans, cycle_dev, pixels = sky_maps.shape
    chan_groups = lax.axis_size("chan")
    blk_groups = lax.axis_size("blk")
    chan, blk = lax.axis_index("chan"), lax.axis_index("blk")
    slot_dev = filters.shape[0]
    degree_count = slot_degree_values.shape[0]
    mode_dev = band_order_values.shape[0] // blk_groups
    cycle_total = cycle_dev * blk_groups
    group_slots = slot_dev * blk_groups
    colatitude = polar_angle_values(cycle_total)
    cycle_factor = (
        2.0 * math.sqrt(2.0 * BAND / cycle_total) * jnp.sin(colatitude) * (1.0 / math.sqrt(pixels))
    )
    local_factor = lax.dynamic_slice_in_dim(cycle_factor, blk * cycle_dev, cycle_dev)
    local_modes = lax.dynamic_slice_in_dim(band_order_values, blk * mode_dev, mode_dev)
    degrees = lax.dynamic_slice_in_dim(slot_degree_values, chan * group_slots, group_slots)

    spectra = analysis(sky_maps, local_factor, band_order_values)
    spectra = spectra.reshape(blk_groups, mode_dev, cycle_dev, 2 * chans)
    spectra = lax.all_to_all(spectra, "blk", split_axis=0, concat_axis=0, tiled=True)
    def swap(value, t):
        return lax.ppermute(value, "chan", [(i, i ^ t) for i in range(chan_groups)])

    def exchange(value):
        return lax.all_to_all(value, "blk", split_axis=0, concat_axis=0, tiled=True)

    near = max(1, chan_groups // 2)
    hops = [[0], list(range(1, near)), list(range(near, chan_groups))]
    hops = [h for h in hops if h]
    counts = [len(h) for h in hops]
    place = jnp.arange(chan_groups, dtype=jnp.int32) ^ chan
    gathered = [spectra]
    for t in range(1, chan_groups):
        top = 1 << (t.bit_length() - 1)
        gathered.append(swap(gathered[0], t) if t == top else swap(gathered[top], t ^ top))
    lat, turned = legendre(degrees, local_modes, colatitude, degree_count)
    coeffs = []
    for part in hops:
        incoming = [gathered[t] for t in part]
        result = harmonic(lat, incoming, slot_dev)
        if coeffs:
            result, coeffs[-1] = lax.optimization_barrier((result, coeffs[-1]))
        lat, result = lax.optimization_barrier((lat, result))
        coeffs.append(exchange(result))
    scale = 2.0 / math.sqrt(degree_count)
    far = apply_filters(place, filters, coeffs, counts, hops[-1:])
    place, far = lax.optimization_barrier((place, far))
    rest = apply_filters(place, filters, coeffs, counts, hops[-2::-1])
    partial = {}
    for part, filtered in zip(hops[::-1], list(far) + list(rest)):
        partial.update(zip(part, to_cycles(turned, exchange(filtered), scale, blk_groups, len(part))))
    total = partial[0].astype(F32)
    top = chan_groups // 2
    while top:
        group = partial[top].astype(F32)
        for t in range(top + 1, 2 * top):
            group = group + swap(partial[t], t ^ top).astype(F32)
        total = total + swap(group.astype(BF16), top).astype(F32)
        top //= 2
    cycle_part = total.astype(BF16)
    by_cycle = lax.all_to_all(cycle_part, "blk", split_axis=0, concat_axis=0, tiled=True)
    by_cycle = by_cycle.reshape(blk_groups * mode_dev, cycle_dev, 2 * chans)
    return synthesis(by_cycle, band_order_values, pixels)


def solution(mesh):
    in_specs = (P("chan", "blk", None), P(("chan", "blk"), None, None), P(), P())
    out_specs = P("chan", "blk", None)
    return jax.shard_map(body, mesh=mesh, in_specs=in_specs, out_specs=out_specs, check_vma=False)
```

```python
import functools
import math

import jax
import jax.numpy as jnp
from jax import lax
from jax.experimental import pallas as pl
from jax.experimental.pallas import tpu as pltpu
from jax.sharding import PartitionSpec as P

BAND = 0.38
VMEM_LIMIT = 56 * 1024 * 1024
F32 = jnp.float32
BF16 = jnp.bfloat16
COST = pl.CostEstimate(flops=2_000_000_000, bytes_accessed=12_000_000, transcendentals=0)


def params(**kw):
    return pltpu.CompilerParams(vmem_limit_bytes=VMEM_LIMIT, **kw)


def polar_angle_values(cycle_total):
    position = (jnp.arange(cycle_total, dtype=F32) + 0.5) / cycle_total
    return 0.5 * math.pi + BAND * (2.0 * position - 1.0)


def divisor(n, most):
    return max(d for d in range(1, most + 1) if n % d == 0)


def lane_blocks(width):
    return -(-width // 128)


def put(ref, rows, value):
    width = value.shape[1]
    for h in range(ref.shape[0]):
        piece = value[:, h * 128 : min((h + 1) * 128, width)]
        if piece.shape[1] < 128:
            piece = jnp.concatenate([piece, jnp.zeros((piece.shape[0], 128 - piece.shape[1]), piece.dtype)], axis=1)
        ref[h, rows, :] = piece


def get(ref, rows, width):
    value = jnp.concatenate([ref[h, rows, :] for h in range(ref.shape[0])], axis=1)
    return value if width == value.shape[1] else value[:, :width]


def analysis_kernel(steps, factor_ref, modes_ref, sky_ref, out_ref, phase_ref, prod_ref, turn_ref):
    step = pl.program_id(0)
    chans, cycles, pixels = sky_ref.shape
    modes = modes_ref.shape[1]
    low = 64
    high = pixels // low

    @pl.when(step == 0)
    def _():
        ids = modes_ref[...]
        unit = 2.0 * math.pi / pixels

        def table(rows, stride):
            index = lax.broadcasted_iota(jnp.int32, (rows, modes), 0) * stride
            angle = unit * ((index * ids) & (pixels - 1)).astype(F32)
            return jnp.cos(angle), jnp.sin(angle)

        cos_low, sin_low = table(low, 1)
        cos_high, sin_high = table(high, low)
        for h in range(high):
            ca, sa = cos_high[h : h + 1], sin_high[h : h + 1]
            rows = slice(h * low, (h + 1) * low)
            phase_ref[rows, :modes] = (ca * cos_low - sa * sin_low).astype(BF16)
            phase_ref[rows, modes:] = (-(sa * cos_low + ca * sin_low)).astype(BF16)

    rows = chans * cycles
    product = jnp.dot(sky_ref[...].reshape(rows, pixels), phase_ref[...], preferred_element_type=F32)
    put(prod_ref, pl.ds(pl.multiple_of(step * rows, rows), rows), product)

    @pl.when(step == steps - 1)
    def _():
        total = chans * steps
        for r in range(cycles):
            part = get(prod_ref, pl.ds(r, total, stride=cycles), 2 * modes) * factor_ref[r]
            both = [part[:, k * modes : (k + 1) * modes].T for k in range(2)]
            put(turn_ref, pl.ds(r, modes, stride=cycles), jnp.concatenate(both, axis=1))
        out_ref[...] = get(turn_ref, slice(None), 2 * total).astype(BF16).reshape(out_ref.shape)


def analysis(sky, factor, modes):
    chans, cycles, pixels = sky.shape
    count = modes.shape[0]
    steps = divisor(chans, 2)
    return pl.pallas_call(
        functools.partial(analysis_kernel, steps),
        grid=(steps,),
        in_specs=[
            pl.BlockSpec(memory_space=pltpu.SMEM),
            pl.BlockSpec((1, count), lambda i: (0, 0)),
            pl.BlockSpec((chans // steps, cycles, pixels), lambda i: (i, 0, 0)),
        ],
        out_specs=pl.BlockSpec((count, cycles, 2 * chans), lambda i: (0, 0, 0)),
        out_shape=jax.ShapeDtypeStruct((count, cycles, 2 * chans), BF16),
        scratch_shapes=[
            pltpu.VMEM((pixels, 2 * count), BF16),
            pltpu.VMEM((lane_blocks(2 * count), chans * cycles, 128), F32),
            pltpu.VMEM((lane_blocks(2 * chans), count * cycles, 128), F32),
        ],
        compiler_params=params(),
        name="analysis",
    )(factor, modes.reshape(1, count), sky)


def legendre_kernel(levels, first_ref, degree_ref, band_ref, log_ref, lat_ref, turned_ref, gain_ref, all_ref, pick_ref):
    modes, slots, cycles = lat_ref.shape
    block = 128
    row = lax.broadcasted_iota(jnp.int32, (modes, 1), 0)
    order = jnp.zeros((modes, 1), F32)
    log_seed = jnp.zeros((modes, 1), F32)
    for j in range(modes):
        order = jnp.where(row == j, band_ref[first_ref[0] + j].astype(F32), order)
        log_seed = jnp.where(row == j, log_ref[first_ref[0] + j], log_seed)
    level = lax.broadcasted_iota(jnp.int32, (modes, levels), 1).astype(F32)
    squared = order * order

    def growth(n):
        return jnp.sqrt(jnp.maximum(4.0 * n * n - 1.0, 1.0) / jnp.maximum(n * n - squared, 1.0))

    here = growth(level)
    gain_ref[0] = here
    gain_ref[1] = here / growth(level - 1.0)
    position = (lax.broadcasted_iota(jnp.int32, (1, cycles), 1).astype(F32) + 0.5) / cycles
    colatitude = 0.5 * math.pi + BAND * (2.0 * position - 1.0)
    cosine = jnp.broadcast_to(jnp.cos(colatitude), (modes, cycles))
    orders = jnp.broadcast_to(order, (modes, cycles))
    seed = jnp.exp(log_seed + order * jnp.log(jnp.sin(colatitude)))

    def advance(i, carry):
        latest, earlier = carry
        start = pl.multiple_of(i * block, block)
        first = gain_ref[0, :, pl.ds(start, block)]
        second = gain_ref[1, :, pl.ds(start, block)]
        base = (i * block).astype(F32)
        for n in range(block):
            up = jnp.broadcast_to(first[:, n : n + 1], (modes, cycles)) * cosine
            down = jnp.broadcast_to(second[:, n : n + 1], (modes, cycles))
            begin = jnp.where(orders == base + n, seed, 0.0)
            current = up * latest + (begin - down * earlier)
            put(all_ref, pl.ds(pl.multiple_of((start + n) * modes, modes), modes), current)
            latest, earlier = current, latest
        return latest, earlier

    zero = jnp.zeros((modes, cycles), F32)
    lax.fori_loop(0, levels // block, advance, (zero, zero))

    def pick(s, _):
        source = pl.multiple_of(degree_ref[first_ref[1] + s] * modes, modes)
        for h in range(all_ref.shape[0]):
            pick_ref[h, pl.ds(pl.multiple_of(s * modes, modes), modes), :] = all_ref[h, pl.ds(source, modes), :]
        return 0

    lax.fori_loop(0, slots, pick, 0, unroll=8)
    for j in range(modes):
        rows = get(pick_ref, pl.ds(j, slots, stride=modes), cycles)
        lat_ref[j] = rows.astype(BF16)
        turned_ref[j] = rows.T.astype(BF16)


def legendre(first, degrees, band, modes, slots, cycles):
    levels = degrees.shape[0]
    m = band.astype(F32)
    log_seed = 0.5 * (
        jnp.log(m + 0.5) + lax.lgamma(m + 0.5) - lax.lgamma(m + 1.0) - 0.5 * math.log(math.pi)
    )
    vmem = pl.BlockSpec(memory_space=pltpu.VMEM)
    return pl.pallas_call(
        functools.partial(legendre_kernel, levels),
        in_specs=[pl.BlockSpec(memory_space=pltpu.SMEM)] * 4,
        out_specs=[vmem, vmem],
        out_shape=[
            jax.ShapeDtypeStruct((modes, slots, cycles), BF16),
            jax.ShapeDtypeStruct((modes, cycles, slots), BF16),
        ],
        scratch_shapes=[
            pltpu.VMEM((2, modes, levels), F32),
            pltpu.VMEM((lane_blocks(cycles), levels * modes, 128), F32),
            pltpu.VMEM((lane_blocks(cycles), slots * modes, 128), F32),
        ],
        compiler_params=params(),
        cost_estimate=pl.CostEstimate(flops=40_000_000, bytes_accessed=30_000_000, transcendentals=0),
        name="legendre",
    )(first, degrees, band, log_seed)


def arrange(pieces, low):
    placed = []
    for p in range(len(pieces)):
        value = pieces[p]
        for q in range(1, len(pieces)):
            value = lax.select(low == q, pieces[p ^ q], value)
        placed.append(value)
    return placed


def by_part(placed, chans):
    return [jnp.concatenate([p[:, k * chans : (k + 1) * chans] for p in placed], axis=1) for k in range(2)]


def harmonic_kernel(counts, family, low_ref, lat_ref, *refs):
    spectra, out_ref, turn_ref = refs[: sum(counts)], *refs[sum(counts) :]
    _, modes, cycles, pair = spectra[0].shape
    slots = out_ref.shape[0] * out_ref.shape[1]
    width = out_ref.shape[3]
    for j in range(modes):
        rights = []
        first = 0
        for count in counts:
            pieces = [p[:, j].reshape(p.shape[0] * cycles, pair) for p in spectra[first : first + count]]
            rights.append(pieces[0] if count == 1 else jnp.concatenate(pieces, axis=0))
            first += count
        if family:
            rights = by_part(arrange(rights, low_ref[0]), pair // 2)
        right = rights[0] if len(rights) == 1 else jnp.concatenate(rights, axis=1)
        result = jnp.dot(lat_ref[j], right, preferred_element_type=F32)
        put(turn_ref, pl.ds(j, slots, stride=modes), result)
    out_ref[...] = get(turn_ref, slice(None), width).astype(BF16).reshape(out_ref.shape)


def harmonic(low, lat, spectra, slot_dev, family):
    modes, slots, cycle_total = lat.shape
    _, _, cycles, pair = spectra[0][0].shape
    counts = [len(pieces) for pieces in spectra]
    pieces = sum(spectra, [])
    width = len(spectra) * pair
    dests = slots // slot_dev
    steps = divisor(dests, 2)
    return pl.pallas_call(
        functools.partial(harmonic_kernel, counts, family),
        grid=(steps,),
        in_specs=[
            pl.BlockSpec(memory_space=pltpu.SMEM),
            pl.BlockSpec((modes, slots // steps, cycle_total), lambda i: (0, i, 0)),
        ]
        + [pl.BlockSpec(p.shape, lambda i: (0, 0, 0, 0)) for p in pieces],
        out_specs=pl.BlockSpec((dests // steps, slot_dev, modes, width), lambda i: (i, 0, 0, 0)),
        out_shape=jax.ShapeDtypeStruct((dests, slot_dev, modes, width), BF16),
        scratch_shapes=[pltpu.VMEM((lane_blocks(width), slots // steps * modes, 128), F32)],
        compiler_params=params(),
        cost_estimate=COST,
        name="harmonic",
    )(low, lat, *pieces)


def filter_kernel(counts, wanted, low_ref, filters_ref, *refs):
    inputs, outs, turn_ref = refs[: len(counts)], refs[len(counts) : -1], refs[-1]
    groups, slots, modes, _ = inputs[0].shape
    pair = inputs[0].shape[3] // counts[0]
    chans = pair // 2
    rows = groups * modes
    total = filters_ref.shape[2]
    low, high = low_ref[0], low_ref[1]
    families = total // chans // sum(counts[:2]) if len(counts) > 1 else 1
    width = total // families
    own = pl.multiple_of(high * width, width)
    other = pl.multiple_of((1 - high) * width, width)
    for s in range(slots):
        pieces = []
        for ref, count in zip(inputs[:2], counts):
            pieces += [ref[:, s, :, i * pair : (i + 1) * pair].reshape(rows, pair) for i in range(count)]
        left = jnp.concatenate(by_part(arrange(pieces, low), chans), axis=0)
        if families > 1:
            far = [inputs[2][:, s, :, k * width : (k + 1) * width].reshape(rows, width) for k in range(2)]
            left = jnp.concatenate([left, jnp.concatenate(far, axis=0)], axis=1)
        lane = 0
        for family, hops in wanted:
            if family:
                start, count = other, width
            else:
                start, count = pl.multiple_of(own + (low ^ hops) * chans, chans), chans
            right = filters_ref[s, pl.ds(start, count), pl.ds(own, width)]
            if families > 1:
                right = jnp.concatenate([right, filters_ref[s, pl.ds(start, count), pl.ds(other, width)]], axis=1)
            result = lax.dot_general(left, right, (((1,), (1,)), ((), ())), preferred_element_type=F32)
            result = jnp.concatenate([result[:rows], result[rows:]], axis=1)
            blocks = lane_blocks(2 * count)
            put(turn_ref.at[lane : lane + blocks], pl.ds(s, rows, stride=slots), result)
            lane += blocks
    lane = 0
    for (family, hops), ref in zip(wanted, outs):
        blocks = lane_blocks(ref.shape[3])
        value = get(turn_ref.at[lane : lane + blocks], slice(None), ref.shape[3])
        ref[...] = value.astype(BF16).reshape(ref.shape)
        lane += blocks


def apply_filters(place, filters, coeffs, counts, wanted):
    groups, slots, modes, _ = coeffs[0].shape
    total = filters.shape[2]
    pair = coeffs[0].shape[3] // counts[0]
    step = min(slots, 16)
    widths = [counts[-1] * pair if family else pair for family, _ in wanted]
    return pl.pallas_call(
        functools.partial(filter_kernel, counts, wanted),
        grid=(slots // step,),
        in_specs=[
            pl.BlockSpec(memory_space=pltpu.SMEM),
            pl.BlockSpec((step, total, total), lambda i: (i, 0, 0)),
        ]
        + [pl.BlockSpec((groups, step, modes, c.shape[3]), lambda i: (0, i, 0, 0)) for c in coeffs],
        out_specs=[pl.BlockSpec((groups, modes, step, w), lambda i: (0, 0, i, 0)) for w in widths],
        out_shape=[jax.ShapeDtypeStruct((groups, modes, slots, w), BF16) for w in widths],
        scratch_shapes=[pltpu.VMEM((sum(lane_blocks(w) for w in widths), groups * modes * step, 128), F32)],
        compiler_params=params(),
        cost_estimate=COST,
        name="filters",
    )(place, filters, *coeffs)


def cycles_kernel(scale, low_ref, turned_ref, filtered_ref, *outs):
    groups, modes, slot_dev, width = filtered_ref.shape
    blocks, _, cycles, pair = outs[0].shape
    chans = pair // 2
    parts = len(outs)
    for j in range(modes):
        result = jnp.dot(
            turned_ref[j],
            filtered_ref[:, j].reshape(groups * slot_dev, width),
            preferred_element_type=F32,
        )
        result = result * scale
        if parts == 1:
            pieces = [result]
        else:
            half = width // 2
            pieces = [
                jnp.concatenate([result[:, k * half + p * chans : k * half + (p + 1) * chans] for k in range(2)], axis=1)
                for p in range(parts)
            ]
            pieces = arrange(pieces, low_ref[0])
        for piece, ref in zip(pieces, outs):
            ref[:, j] = piece.astype(BF16).reshape(blocks, cycles, pair)


def to_cycles(low, turned, filtered, scale, blocks, parts):
    modes, cycle_total, slots = turned.shape
    width = filtered.shape[3]
    vmem = pl.BlockSpec(memory_space=pltpu.VMEM)
    shape = (blocks, modes, cycle_total // blocks, width // parts)
    return pl.pallas_call(
        functools.partial(cycles_kernel, scale),
        in_specs=[pl.BlockSpec(memory_space=pltpu.SMEM), vmem, vmem],
        out_specs=[vmem] * parts,
        out_shape=[jax.ShapeDtypeStruct(shape, BF16)] * parts,
        compiler_params=params(),
        cost_estimate=COST,
        name="cycles",
    )(low, turned, filtered)


def synthesis_kernel(modes_ref, parts_ref, out_ref, there_ref, phase_ref, wide_ref, turn_ref, left_ref, sent):
    chans, cycles, pixels = there_ref.shape
    steps = sent.shape[0]
    modes, _, pair = parts_ref.shape
    low = 128
    total = pair // 2
    ids = modes_ref[...]
    unit = 2.0 * math.pi / pixels

    def table(columns, stride):
        index = lax.broadcasted_iota(jnp.int32, (modes, columns), 1) * stride
        angle = unit * ((index * ids) & (pixels - 1)).astype(F32)
        return jnp.cos(angle), jnp.sin(angle)

    cos_low, sin_low = table(low, 1)
    cos_high, sin_high = table(pixels // low, low)
    for h in range(pixels // low):
        ca, sa = cos_high[:, h : h + 1], sin_high[:, h : h + 1]
        columns = slice(h * low, (h + 1) * low)
        phase_ref[:modes, columns] = (ca * cos_low - sa * sin_low).astype(BF16)
        phase_ref[modes:, columns] = (-(sa * cos_low + ca * sin_low)).astype(BF16)
    put(wide_ref, slice(None), parts_ref[...].astype(F32).reshape(modes * cycles, pair))
    for r in range(cycles):
        part = get(wide_ref, pl.ds(r, modes, stride=cycles), pair)
        both = [part[:, k * total : (k + 1) * total].T for k in range(2)]
        put(turn_ref, pl.ds(r, total, stride=cycles), jnp.concatenate(both, axis=1))
    left_ref[...] = get(turn_ref, slice(None), 2 * modes).astype(BF16)

    part = chans // steps
    rows = part * cycles
    copies = []
    for i in range(steps):
        left = left_ref[i * rows : (i + 1) * rows, :]
        result = jnp.dot(left, phase_ref[...], preferred_element_type=F32) * (1.0 / math.sqrt(modes))
        there_ref[i * part : (i + 1) * part] = result.astype(BF16).reshape(part, cycles, pixels)
        window = pl.ds(i * part, part)
        copies.append(pltpu.make_async_copy(there_ref.at[window], out_ref.at[window], sent.at[i]))
        copies[i].start()
    for copy in copies:
        copy.wait()


def synthesis(parts, modes, pixels):
    count, cycles, pair = parts.shape
    chans = pair // 2
    steps = divisor(chans, 8)
    vmem = pl.BlockSpec(memory_space=pltpu.VMEM)
    return pl.pallas_call(
        synthesis_kernel,
        in_specs=[vmem, vmem],
        out_specs=pl.BlockSpec(memory_space=pl.ANY),
        out_shape=jax.ShapeDtypeStruct((chans, cycles, pixels), BF16),
        scratch_shapes=[
            pltpu.VMEM((chans, cycles, pixels), BF16),
            pltpu.VMEM((2 * count, pixels), BF16),
            pltpu.VMEM((lane_blocks(pair), count * cycles, 128), F32),
            pltpu.VMEM((lane_blocks(2 * count), chans * cycles, 128), F32),
            pltpu.VMEM((chans * cycles, 2 * count), BF16),
            pltpu.SemaphoreType.DMA((steps,)),
        ],
        compiler_params=params(),
        name="synthesis",
    )(modes.reshape(count, 1), parts)


def body(sky_maps, filters, band_order_values, slot_degree_values):
    chans, cycle_dev, pixels = sky_maps.shape
    chan_groups = lax.axis_size("chan")
    blk_groups = lax.axis_size("blk")
    chan, blk = lax.axis_index("chan"), lax.axis_index("blk")
    slot_dev = filters.shape[0]
    degree_count = slot_degree_values.shape[0]
    mode_dev = band_order_values.shape[0] // blk_groups
    cycle_total = cycle_dev * blk_groups
    group_slots = slot_dev * blk_groups
    colatitude = polar_angle_values(cycle_total)
    cycle_factor = (
        2.0 * math.sqrt(2.0 * BAND / cycle_total) * jnp.sin(colatitude) * (1.0 / math.sqrt(pixels))
    )
    local_factor = lax.dynamic_slice_in_dim(cycle_factor, blk * cycle_dev, cycle_dev)
    spectra = analysis(sky_maps, local_factor, band_order_values)
    spectra = spectra.reshape(blk_groups, mode_dev, cycle_dev, 2 * chans)
    def swap(value, t):
        return lax.ppermute(value, "chan", [(i, i ^ t) for i in range(chan_groups)])

    def exchange(value):
        return lax.all_to_all(value, "blk", split_axis=0, concat_axis=0, tiled=True)

    near = max(1, chan_groups // 2)
    hops = [[0], list(range(1, near)), list(range(near, chan_groups))]
    hops = [h for h in hops if h]
    counts = [len(h) for h in hops]
    place = jnp.stack([chan % near, chan // near])
    first = jnp.stack([blk * mode_dev, chan * group_slots])
    lat, turned = legendre(first, slot_degree_values, band_order_values, mode_dev, group_slots, cycle_total)
    own = exchange(spectra)
    gathered = [[own]]
    half = max(1, blk_groups * 4 // 8)
    if chan_groups > 1:
        beside = swap(spectra, 1)
        beside, lat, own = lax.optimization_barrier((beside, lat, own))
        beside = exchange(beside)
        gathered = [[own], [beside]]
    for t in range(2, chan_groups):
        top = 1 << (t.bit_length() - 1)
        source = [own[:half], own[half:]] if t == top else gathered[top]
        gathered.append([swap(piece, t if t == top else t ^ top) for piece in source])
    coeffs = []
    for n, part in enumerate(hops):
        result = harmonic(place, lat, [gathered[t] for t in part], slot_dev, n == 2)
        if n == 0 and chan_groups > 1:
            result, gathered[1][0] = lax.optimization_barrier((result, gathered[1][0]))
            if chan_groups > 2:
                result, gathered[2][0] = lax.optimization_barrier((result, gathered[2][0]))
        if n == 1:
            result, coeffs[0] = lax.optimization_barrier((result, coeffs[0]))
            if chan_groups > 2:
                result, gathered[2][1], gathered[3][0] = lax.optimization_barrier((result, gathered[2][1], gathered[3][0]))
        if n == 2:
            result, coeffs[1] = lax.optimization_barrier((result, coeffs[1]))
        lat, result = lax.optimization_barrier((lat, result))
        coeffs.append(exchange(result))
    scale = 2.0 / math.sqrt(degree_count)
    partial = {}
    tasks = [[(False, t)] for part in hops[:2] for t in part][::-1]
    if len(hops) == 3:
        tasks = [[(True, None)]] + [sum(tasks, [])]
    else:
        tasks = [sum(tasks, [])]
    for n, task in enumerate(tasks):
        results = list(apply_filters(place, filters, coeffs, counts, task))
        place, results[0] = lax.optimization_barrier((place, results[0]))
        for (family, t), filtered in zip(task, results):
            names = hops[2] if family else [t]
            outs = to_cycles(place, turned, exchange(filtered), scale, blk_groups, len(names))
            partial.update(zip(names, outs))
    total = partial[0].astype(F32)
    top = chan_groups // 2
    while top:
        group = partial[top].astype(F32)
        for t in range(top + 1, 2 * top):
            group = group + swap(partial[t], t ^ top).astype(F32)
        total = total + swap(group.astype(BF16), top).astype(F32)
        top //= 2
    cycle_part = total.astype(BF16)
    by_cycle = lax.all_to_all(cycle_part, "blk", split_axis=0, concat_axis=0, tiled=True)
    by_cycle = by_cycle.reshape(blk_groups * mode_dev, cycle_dev, 2 * chans)
    return synthesis(by_cycle, band_order_values, pixels)


def solution(mesh):
    in_specs = (P("chan", "blk", None), P(("chan", "blk"), None, None), P(), P())
    out_specs = P("chan", "blk", None)
    return jax.shard_map(body, mesh=mesh, in_specs=in_specs, out_specs=out_specs, check_vma=False)
```

```python
import functools
import math

import jax
import jax.numpy as jnp
from jax import lax
from jax.experimental import pallas as pl
from jax.experimental.pallas import tpu as pltpu
from jax.sharding import PartitionSpec as P

BAND = 0.38
VMEM_LIMIT = 56 * 1024 * 1024
F32 = jnp.float32
BF16 = jnp.bfloat16
COST = pl.CostEstimate(flops=2_000_000_000, bytes_accessed=12_000_000, transcendentals=0)


def params(**kw):
    return pltpu.CompilerParams(vmem_limit_bytes=VMEM_LIMIT, **kw)


def polar_angle_values(cycle_total):
    position = (jnp.arange(cycle_total, dtype=F32) + 0.5) / cycle_total
    return 0.5 * math.pi + BAND * (2.0 * position - 1.0)


def divisor(n, most):
    return max(d for d in range(1, most + 1) if n % d == 0)


def lane_blocks(width):
    return -(-width // 128)


def put(ref, rows, value):
    width = value.shape[1]
    for h in range(ref.shape[0]):
        piece = value[:, h * 128 : min((h + 1) * 128, width)]
        if piece.shape[1] < 128:
            piece = jnp.concatenate([piece, jnp.zeros((piece.shape[0], 128 - piece.shape[1]), piece.dtype)], axis=1)
        ref[h, rows, :] = piece


def get(ref, rows, width):
    value = jnp.concatenate([ref[h, rows, :] for h in range(ref.shape[0])], axis=1)
    return value if width == value.shape[1] else value[:, :width]


def analysis_kernel(steps, factor_ref, modes_ref, sky_ref, out_ref, phase_ref, prod_ref, turn_ref):
    step = pl.program_id(0)
    chans, cycles, pixels = sky_ref.shape
    modes = modes_ref.shape[1]
    low = 64
    high = pixels // low

    @pl.when(step == 0)
    def _():
        ids = modes_ref[...]
        unit = 2.0 * math.pi / pixels

        def table(rows, stride):
            index = lax.broadcasted_iota(jnp.int32, (rows, modes), 0) * stride
            angle = unit * ((index * ids) & (pixels - 1)).astype(F32)
            return jnp.cos(angle), jnp.sin(angle)

        cos_low, sin_low = table(low, 1)
        cos_high, sin_high = table(high, low)
        for h in range(high):
            ca, sa = cos_high[h : h + 1], sin_high[h : h + 1]
            rows = slice(h * low, (h + 1) * low)
            phase_ref[rows, :modes] = (ca * cos_low - sa * sin_low).astype(BF16)
            phase_ref[rows, modes:] = (-(sa * cos_low + ca * sin_low)).astype(BF16)

    rows = chans * cycles
    product = jnp.dot(sky_ref[...].reshape(rows, pixels), phase_ref[...], preferred_element_type=F32)
    put(prod_ref, pl.ds(pl.multiple_of(step * rows, rows), rows), product)

    @pl.when(step == steps - 1)
    def _():
        total = chans * steps
        for r in range(cycles):
            part = get(prod_ref, pl.ds(r, total, stride=cycles), 2 * modes) * factor_ref[r]
            both = [part[:, k * modes : (k + 1) * modes].T for k in range(2)]
            put(turn_ref, pl.ds(r, modes, stride=cycles), jnp.concatenate(both, axis=1))
        out_ref[...] = get(turn_ref, slice(None), 2 * total).astype(BF16).reshape(out_ref.shape)


def analysis(sky, factor, modes):
    chans, cycles, pixels = sky.shape
    count = modes.shape[0]
    steps = divisor(chans, 2)
    return pl.pallas_call(
        functools.partial(analysis_kernel, steps),
        grid=(steps,),
        in_specs=[
            pl.BlockSpec(memory_space=pltpu.SMEM),
            pl.BlockSpec((1, count), lambda i: (0, 0)),
            pl.BlockSpec((chans // steps, cycles, pixels), lambda i: (i, 0, 0)),
        ],
        out_specs=pl.BlockSpec((count, cycles, 2 * chans), lambda i: (0, 0, 0)),
        out_shape=jax.ShapeDtypeStruct((count, cycles, 2 * chans), BF16),
        scratch_shapes=[
            pltpu.VMEM((pixels, 2 * count), BF16),
            pltpu.VMEM((lane_blocks(2 * count), chans * cycles, 128), F32),
            pltpu.VMEM((lane_blocks(2 * chans), count * cycles, 128), F32),
        ],
        compiler_params=params(),
        name="analysis",
    )(factor, modes.reshape(1, count), sky)


def legendre_kernel(levels, first_ref, degree_ref, band_ref, log_ref, lat_ref, turned_ref, gain_ref, all_ref, pick_ref):
    modes, slots, cycles = lat_ref.shape
    block = 128
    row = lax.broadcasted_iota(jnp.int32, (modes, 1), 0)
    order = jnp.zeros((modes, 1), F32)
    log_seed = jnp.zeros((modes, 1), F32)
    for j in range(modes):
        order = jnp.where(row == j, band_ref[first_ref[0] + j].astype(F32), order)
        log_seed = jnp.where(row == j, log_ref[first_ref[0] + j], log_seed)
    level = lax.broadcasted_iota(jnp.int32, (modes, levels), 1).astype(F32)
    squared = order * order

    def growth(n):
        return jnp.sqrt(jnp.maximum(4.0 * n * n - 1.0, 1.0) / jnp.maximum(n * n - squared, 1.0))

    here = growth(level)
    gain_ref[0] = here
    gain_ref[1] = here / growth(level - 1.0)
    position = (lax.broadcasted_iota(jnp.int32, (1, cycles), 1).astype(F32) + 0.5) / cycles
    colatitude = 0.5 * math.pi + BAND * (2.0 * position - 1.0)
    cosine = jnp.broadcast_to(jnp.cos(colatitude), (modes, cycles))
    orders = jnp.broadcast_to(order, (modes, cycles))
    seed = jnp.exp(log_seed + order * jnp.log(jnp.sin(colatitude)))

    def advance(i, carry):
        latest, earlier = carry
        start = pl.multiple_of(i * block, block)
        first = gain_ref[0, :, pl.ds(start, block)]
        second = gain_ref[1, :, pl.ds(start, block)]
        base = (i * block).astype(F32)
        for n in range(block):
            up = jnp.broadcast_to(first[:, n : n + 1], (modes, cycles)) * cosine
            down = jnp.broadcast_to(second[:, n : n + 1], (modes, cycles))
            begin = jnp.where(orders == base + n, seed, 0.0)
            current = up * latest + (begin - down * earlier)
            put(all_ref, pl.ds(pl.multiple_of((start + n) * modes, modes), modes), current)
            latest, earlier = current, latest
        return latest, earlier

    zero = jnp.zeros((modes, cycles), F32)
    lax.fori_loop(0, levels // block, advance, (zero, zero))

    def pick(s, _):
        source = pl.multiple_of(degree_ref[first_ref[1] + s] * modes, modes)
        for h in range(all_ref.shape[0]):
            pick_ref[h, pl.ds(pl.multiple_of(s * modes, modes), modes), :] = all_ref[h, pl.ds(source, modes), :]
        return 0

    lax.fori_loop(0, slots, pick, 0, unroll=8)
    for j in range(modes):
        rows = get(pick_ref, pl.ds(j, slots, stride=modes), cycles)
        lat_ref[j] = rows.astype(BF16)
        turned_ref[j] = rows.T.astype(BF16)


def legendre(first, degrees, band, modes, slots, cycles):
    levels = degrees.shape[0]
    m = band.astype(F32)
    log_seed = 0.5 * (
        jnp.log(m + 0.5) + lax.lgamma(m + 0.5) - lax.lgamma(m + 1.0) - 0.5 * math.log(math.pi)
    )
    vmem = pl.BlockSpec(memory_space=pltpu.VMEM)
    return pl.pallas_call(
        functools.partial(legendre_kernel, levels),
        in_specs=[pl.BlockSpec(memory_space=pltpu.SMEM)] * 4,
        out_specs=[vmem, vmem],
        out_shape=[
            jax.ShapeDtypeStruct((modes, slots, cycles), BF16),
            jax.ShapeDtypeStruct((modes, cycles, slots), BF16),
        ],
        scratch_shapes=[
            pltpu.VMEM((2, modes, levels), F32),
            pltpu.VMEM((lane_blocks(cycles), levels * modes, 128), F32),
            pltpu.VMEM((lane_blocks(cycles), slots * modes, 128), F32),
        ],
        compiler_params=params(),
        cost_estimate=pl.CostEstimate(flops=40_000_000, bytes_accessed=30_000_000, transcendentals=0),
        name="legendre",
    )(first, degrees, band, log_seed)


def arrange(pieces, low):
    placed = []
    for p in range(len(pieces)):
        value = pieces[p]
        for q in range(1, len(pieces)):
            value = lax.select(low == q, pieces[p ^ q], value)
        placed.append(value)
    return placed


def by_part(placed, chans):
    return [jnp.concatenate([p[:, k * chans : (k + 1) * chans] for p in placed], axis=1) for k in range(2)]


def harmonic_kernel(counts, family, low_ref, lat_ref, *refs):
    spectra, out_ref, turn_ref = refs[: sum(counts)], *refs[sum(counts) :]
    _, modes, cycles, pair = spectra[0].shape
    slots = out_ref.shape[0] * out_ref.shape[1]
    width = out_ref.shape[3]
    for j in range(modes):
        rights = []
        first = 0
        for count in counts:
            pieces = [p[:, j].reshape(p.shape[0] * cycles, pair) for p in spectra[first : first + count]]
            rights.append(pieces[0] if count == 1 else jnp.concatenate(pieces, axis=0))
            first += count
        if family:
            rights = by_part(arrange(rights, low_ref[0]), pair // 2)
        right = rights[0] if len(rights) == 1 else jnp.concatenate(rights, axis=1)
        result = jnp.dot(lat_ref[j], right, preferred_element_type=F32)
        put(turn_ref, pl.ds(j, slots, stride=modes), result)
    out_ref[...] = get(turn_ref, slice(None), width).astype(BF16).reshape(out_ref.shape)


def harmonic(low, lat, spectra, slot_dev, family):
    modes, slots, cycle_total = lat.shape
    _, _, cycles, pair = spectra[0][0].shape
    counts = [len(pieces) for pieces in spectra]
    pieces = sum(spectra, [])
    width = len(spectra) * pair
    dests = slots // slot_dev
    steps = divisor(dests, 2)
    return pl.pallas_call(
        functools.partial(harmonic_kernel, counts, family),
        grid=(steps,),
        in_specs=[
            pl.BlockSpec(memory_space=pltpu.SMEM),
            pl.BlockSpec((modes, slots // steps, cycle_total), lambda i: (0, i, 0)),
        ]
        + [pl.BlockSpec(p.shape, lambda i: (0, 0, 0, 0)) for p in pieces],
        out_specs=pl.BlockSpec((dests // steps, slot_dev, modes, width), lambda i: (i, 0, 0, 0)),
        out_shape=jax.ShapeDtypeStruct((dests, slot_dev, modes, width), BF16),
        scratch_shapes=[pltpu.VMEM((lane_blocks(width), slots // steps * modes, 128), F32)],
        compiler_params=params(),
        cost_estimate=COST,
        name="harmonic",
    )(low, lat, *pieces)


def filter_kernel(counts, wanted, low_ref, filters_ref, *refs):
    inputs, outs, turn_ref = refs[: len(counts)], refs[len(counts) : -1], refs[-1]
    groups, slots, modes, _ = inputs[0].shape
    pair = inputs[0].shape[3] // counts[0]
    chans = pair // 2
    rows = groups * modes
    total = filters_ref.shape[2]
    low, high = low_ref[0], low_ref[1]
    families = total // chans // sum(counts[:2]) if len(counts) > 1 else 1
    width = total // families
    own = pl.multiple_of(high * width, width)
    other = pl.multiple_of((1 - high) * width, width)
    for s in range(slots):
        pieces = []
        for ref, count in zip(inputs[:2], counts):
            pieces += [ref[:, s, :, i * pair : (i + 1) * pair].reshape(rows, pair) for i in range(count)]
        left = jnp.concatenate(by_part(arrange(pieces, low), chans), axis=0)
        if families > 1:
            far = [inputs[2][:, s, :, k * width : (k + 1) * width].reshape(rows, width) for k in range(2)]
            left = jnp.concatenate([left, jnp.concatenate(far, axis=0)], axis=1)
        lane = 0
        for family, hops in wanted:
            if family:
                start, count = other, width
            else:
                start, count = pl.multiple_of(own + (low ^ hops) * chans, chans), chans
            right = filters_ref[s, pl.ds(start, count), pl.ds(own, width)]
            if families > 1:
                right = jnp.concatenate([right, filters_ref[s, pl.ds(start, count), pl.ds(other, width)]], axis=1)
            result = lax.dot_general(left, right, (((1,), (1,)), ((), ())), preferred_element_type=F32)
            result = jnp.concatenate([result[:rows], result[rows:]], axis=1)
            blocks = lane_blocks(2 * count)
            put(turn_ref.at[lane : lane + blocks], pl.ds(s, rows, stride=slots), result)
            lane += blocks
    lane = 0
    for (family, hops), ref in zip(wanted, outs):
        blocks = lane_blocks(ref.shape[3])
        value = get(turn_ref.at[lane : lane + blocks], slice(None), ref.shape[3])
        ref[...] = value.astype(BF16).reshape(ref.shape)
        lane += blocks


def apply_filters(place, filters, coeffs, counts, wanted):
    groups, slots, modes, _ = coeffs[0].shape
    total = filters.shape[2]
    pair = coeffs[0].shape[3] // counts[0]
    step = min(slots, 16)
    widths = [counts[-1] * pair if family else pair for family, _ in wanted]
    return pl.pallas_call(
        functools.partial(filter_kernel, counts, wanted),
        grid=(slots // step,),
        in_specs=[
            pl.BlockSpec(memory_space=pltpu.SMEM),
            pl.BlockSpec((step, total, total), lambda i: (i, 0, 0)),
        ]
        + [pl.BlockSpec((groups, step, modes, c.shape[3]), lambda i: (0, i, 0, 0)) for c in coeffs],
        out_specs=[pl.BlockSpec((groups, modes, step, w), lambda i: (0, 0, i, 0)) for w in widths],
        out_shape=[jax.ShapeDtypeStruct((groups, modes, slots, w), BF16) for w in widths],
        scratch_shapes=[pltpu.VMEM((sum(lane_blocks(w) for w in widths), groups * modes * step, 128), F32)],
        compiler_params=params(),
        cost_estimate=COST,
        name="filters",
    )(place, filters, *coeffs)


def cycles_kernel(scale, low_ref, turned_ref, filtered_ref, *outs):
    groups, modes, slot_dev, width = filtered_ref.shape
    blocks, _, cycles, pair = outs[0].shape
    chans = pair // 2
    parts = len(outs)
    for j in range(modes):
        result = jnp.dot(
            turned_ref[j],
            filtered_ref[:, j].reshape(groups * slot_dev, width),
            preferred_element_type=F32,
        )
        result = result * scale
        if parts == 1:
            pieces = [result]
        else:
            half = width // 2
            pieces = [
                jnp.concatenate([result[:, k * half + p * chans : k * half + (p + 1) * chans] for k in range(2)], axis=1)
                for p in range(parts)
            ]
            pieces = arrange(pieces, low_ref[0])
        for piece, ref in zip(pieces, outs):
            ref[:, j] = piece.astype(BF16).reshape(blocks, cycles, pair)


def to_cycles(low, turned, filtered, scale, blocks, parts):
    modes, cycle_total, slots = turned.shape
    width = filtered.shape[3]
    vmem = pl.BlockSpec(memory_space=pltpu.VMEM)
    shape = (blocks, modes, cycle_total // blocks, width // parts)
    return pl.pallas_call(
        functools.partial(cycles_kernel, scale),
        in_specs=[pl.BlockSpec(memory_space=pltpu.SMEM), vmem, vmem],
        out_specs=[vmem] * parts,
        out_shape=[jax.ShapeDtypeStruct(shape, BF16)] * parts,
        compiler_params=params(),
        cost_estimate=COST,
        name="cycles",
    )(low, turned, filtered)


def phases_kernel(modes_ref, phase_ref):
    modes, pixels = modes_ref.shape[0], phase_ref.shape[1]
    low = 128
    ids = modes_ref[...]
    unit = 2.0 * math.pi / pixels

    def table(columns, stride):
        index = lax.broadcasted_iota(jnp.int32, (modes, columns), 1) * stride
        angle = unit * ((index * ids) & (pixels - 1)).astype(F32)
        return jnp.cos(angle), jnp.sin(angle)

    cos_low, sin_low = table(low, 1)
    cos_high, sin_high = table(pixels // low, low)
    for h in range(pixels // low):
        ca, sa = cos_high[:, h : h + 1], sin_high[:, h : h + 1]
        columns = slice(h * low, (h + 1) * low)
        phase_ref[:modes, columns] = (ca * cos_low - sa * sin_low).astype(BF16)
        phase_ref[modes:, columns] = (-(sa * cos_low + ca * sin_low)).astype(BF16)


def phases_of(modes, pixels):
    count = modes.shape[0]
    vmem = pl.BlockSpec(memory_space=pltpu.VMEM)
    return pl.pallas_call(
        phases_kernel,
        in_specs=[vmem],
        out_specs=vmem,
        out_shape=jax.ShapeDtypeStruct((2 * count, pixels), BF16),
        compiler_params=params(),
        cost_estimate=COST,
        name="phases",
    )(modes.reshape(count, 1))


def synthesis_kernel(phase_ref, parts_ref, out_ref, there_ref, wide_ref, turn_ref, left_ref, sent):
    chans, cycles, pixels = there_ref.shape
    steps = sent.shape[0]
    modes, _, pair = parts_ref.shape
    total = pair // 2
    put(wide_ref, slice(None), parts_ref[...].astype(F32).reshape(modes * cycles, pair))
    for r in range(cycles):
        part = get(wide_ref, pl.ds(r, modes, stride=cycles), pair)
        both = [part[:, k * total : (k + 1) * total].T for k in range(2)]
        put(turn_ref, pl.ds(r, total, stride=cycles), jnp.concatenate(both, axis=1))
    left_ref[...] = get(turn_ref, slice(None), 2 * modes).astype(BF16)

    part = chans // steps
    rows = part * cycles
    copies = []
    for i in range(steps):
        left = left_ref[i * rows : (i + 1) * rows, :]
        result = jnp.dot(left, phase_ref[...], preferred_element_type=F32) * (1.0 / math.sqrt(modes))
        there_ref[i * part : (i + 1) * part] = result.astype(BF16).reshape(part, cycles, pixels)
        window = pl.ds(i * part, part)
        copies.append(pltpu.make_async_copy(there_ref.at[window], out_ref.at[window], sent.at[i]))
        copies[i].start()
    for copy in copies:
        copy.wait()


def synthesis(parts, phases):
    count, cycles, pair = parts.shape
    pixels = phases.shape[1]
    chans = pair // 2
    steps = divisor(chans, 8)
    vmem = pl.BlockSpec(memory_space=pltpu.VMEM)
    return pl.pallas_call(
        synthesis_kernel,
        in_specs=[vmem, vmem],
        out_specs=pl.BlockSpec(memory_space=pl.ANY),
        out_shape=jax.ShapeDtypeStruct((chans, cycles, pixels), BF16),
        scratch_shapes=[
            pltpu.VMEM((chans, cycles, pixels), BF16),
            pltpu.VMEM((lane_blocks(pair), count * cycles, 128), F32),
            pltpu.VMEM((lane_blocks(2 * count), chans * cycles, 128), F32),
            pltpu.VMEM((chans * cycles, 2 * count), BF16),
            pltpu.SemaphoreType.DMA((steps,)),
        ],
        compiler_params=params(),
        name="synthesis",
    )(phases, parts)


def body(sky_maps, filters, band_order_values, slot_degree_values):
    chans, cycle_dev, pixels = sky_maps.shape
    chan_groups = lax.axis_size("chan")
    blk_groups = lax.axis_size("blk")
    chan, blk = lax.axis_index("chan"), lax.axis_index("blk")
    slot_dev = filters.shape[0]
    degree_count = slot_degree_values.shape[0]
    mode_dev = band_order_values.shape[0] // blk_groups
    cycle_total = cycle_dev * blk_groups
    group_slots = slot_dev * blk_groups
    colatitude = polar_angle_values(cycle_total)
    cycle_factor = (
        2.0 * math.sqrt(2.0 * BAND / cycle_total) * jnp.sin(colatitude) * (1.0 / math.sqrt(pixels))
    )
    local_factor = lax.dynamic_slice_in_dim(cycle_factor, blk * cycle_dev, cycle_dev)
    spectra = analysis(sky_maps, local_factor, band_order_values)
    spectra = spectra.reshape(blk_groups, mode_dev, cycle_dev, 2 * chans)
    def swap(value, t):
        return lax.ppermute(value, "chan", [(i, i ^ t) for i in range(chan_groups)])

    def exchange(value):
        return lax.all_to_all(value, "blk", split_axis=0, concat_axis=0, tiled=True)

    near = max(1, chan_groups // 2)
    hops = [[0], list(range(1, near)), list(range(near, chan_groups))]
    hops = [h for h in hops if h]
    counts = [len(h) for h in hops]
    place = jnp.stack([chan % near, chan // near])
    first = jnp.stack([blk * mode_dev, chan * group_slots])
    lat, turned = legendre(first, slot_degree_values, band_order_values, mode_dev, group_slots, cycle_total)
    own = exchange(spectra)
    gathered = [[own]]
    half = max(1, blk_groups * 4 // 8)
    if chan_groups > 1:
        beside = swap(spectra, 1)
        beside, lat, own = lax.optimization_barrier((beside, lat, own))
        beside = exchange(beside)
        gathered = [[own], [beside]]
    for t in range(2, chan_groups):
        top = 1 << (t.bit_length() - 1)
        source = [own[:half], own[half:]] if t == top else gathered[top]
        gathered.append([swap(piece, t if t == top else t ^ top) for piece in source])
    coeffs = []
    for n, part in enumerate(hops):
        result = harmonic(place, lat, [gathered[t] for t in part], slot_dev, n == 2)
        if n == 0 and chan_groups > 1:
            result, gathered[1][0] = lax.optimization_barrier((result, gathered[1][0]))
            if chan_groups > 2:
                result, gathered[2][0] = lax.optimization_barrier((result, gathered[2][0]))
        if n == 1:
            result, coeffs[0] = lax.optimization_barrier((result, coeffs[0]))
            if chan_groups > 2:
                result, gathered[2][1], gathered[3][0] = lax.optimization_barrier((result, gathered[2][1], gathered[3][0]))
        if n == 2:
            result, coeffs[1] = lax.optimization_barrier((result, coeffs[1]))
        lat, result = lax.optimization_barrier((lat, result))
        coeffs.append(exchange(result))
    scale = 2.0 / math.sqrt(degree_count)
    partial = {}
    tasks = [[(False, t)] for part in hops[:2] for t in part][::-1]
    if len(hops) == 3:
        tasks = [[(True, None)]] + [sum(tasks, [])]
    else:
        tasks = [sum(tasks, [])]
    for n, task in enumerate(tasks):
        results = list(apply_filters(place, filters, coeffs, counts, task))
        place, results[0] = lax.optimization_barrier((place, results[0]))
        for (family, t), filtered in zip(task, results):
            names = hops[2] if family else [t]
            outs = to_cycles(place, turned, exchange(filtered), scale, blk_groups, len(names))
            partial.update(zip(names, outs))
    total = partial[0].astype(F32)
    top = chan_groups // 2
    while top:
        group = partial[top].astype(F32)
        for t in range(top + 1, 2 * top):
            group = group + swap(partial[t], t ^ top).astype(F32)
        total = total + swap(group.astype(BF16), top).astype(F32)
        top //= 2
    cycle_part = total.astype(BF16)
    by_cycle = lax.all_to_all(cycle_part, "blk", split_axis=0, concat_axis=0, tiled=True)
    by_cycle = by_cycle.reshape(blk_groups * mode_dev, cycle_dev, 2 * chans)
    return synthesis(by_cycle, phases_of(band_order_values, pixels))


def solution(mesh):
    in_specs = (P("chan", "blk", None), P(("chan", "blk"), None, None), P(), P())
    out_specs = P("chan", "blk", None)
    return jax.shard_map(body, mesh=mesh, in_specs=in_specs, out_specs=out_specs, check_vma=False)
```

```python
import functools
import math

import jax
import jax.numpy as jnp
from jax import lax
from jax.experimental import pallas as pl
from jax.experimental.pallas import tpu as pltpu
from jax.sharding import PartitionSpec as P

BAND = 0.38
VMEM_LIMIT = 52 * 1024 * 1024
F32 = jnp.float32
BF16 = jnp.bfloat16
COST = pl.CostEstimate(flops=2_000_000_000, bytes_accessed=12_000_000, transcendentals=0)


def params(**kw):
    return pltpu.CompilerParams(vmem_limit_bytes=VMEM_LIMIT, **kw)


def polar_angle_values(cycle_total):
    position = (jnp.arange(cycle_total, dtype=F32) + 0.5) / cycle_total
    return 0.5 * math.pi + BAND * (2.0 * position - 1.0)


def divisor(n, most):
    return max(d for d in range(1, most + 1) if n % d == 0)


def lane_blocks(width):
    return -(-width // 128)


def put(ref, rows, value):
    width = value.shape[1]
    for h in range(ref.shape[0]):
        piece = value[:, h * 128 : min((h + 1) * 128, width)]
        if piece.shape[1] < 128:
            piece = jnp.concatenate([piece, jnp.zeros((piece.shape[0], 128 - piece.shape[1]), piece.dtype)], axis=1)
        ref[h, rows, :] = piece


def get(ref, rows, width):
    value = jnp.concatenate([ref[h, rows, :] for h in range(ref.shape[0])], axis=1)
    return value if width == value.shape[1] else value[:, :width]


def analysis_kernel(steps, factor_ref, modes_ref, sky_ref, out_ref, phase_ref, prod_ref, turn_ref):
    step = pl.program_id(0)
    chans, cycles, pixels = sky_ref.shape
    modes = modes_ref.shape[1]
    low = 64
    high = pixels // low

    @pl.when(step == 0)
    def _():
        ids = modes_ref[...]
        unit = 2.0 * math.pi / pixels

        def table(rows, stride):
            index = lax.broadcasted_iota(jnp.int32, (rows, modes), 0) * stride
            angle = unit * ((index * ids) & (pixels - 1)).astype(F32)
            return jnp.cos(angle), jnp.sin(angle)

        cos_low, sin_low = table(low, 1)
        cos_high, sin_high = table(high, low)
        for h in range(high):
            ca, sa = cos_high[h : h + 1], sin_high[h : h + 1]
            rows = slice(h * low, (h + 1) * low)
            phase_ref[rows, :modes] = (ca * cos_low - sa * sin_low).astype(BF16)
            phase_ref[rows, modes:] = (-(sa * cos_low + ca * sin_low)).astype(BF16)

    rows = chans * cycles
    product = jnp.dot(sky_ref[...].reshape(rows, pixels), phase_ref[...], preferred_element_type=F32)
    put(prod_ref, pl.ds(pl.multiple_of(step * rows, rows), rows), product)

    @pl.when(step == steps - 1)
    def _():
        total = chans * steps
        for r in range(cycles):
            part = get(prod_ref, pl.ds(r, total, stride=cycles), 2 * modes) * factor_ref[r]
            both = [part[:, k * modes : (k + 1) * modes].T for k in range(2)]
            put(turn_ref, pl.ds(r, modes, stride=cycles), jnp.concatenate(both, axis=1))
        out_ref[...] = get(turn_ref, slice(None), 2 * total).astype(BF16).reshape(out_ref.shape)


def analysis(sky, factor, modes):
    chans, cycles, pixels = sky.shape
    count = modes.shape[0]
    steps = divisor(chans, 2)
    return pl.pallas_call(
        functools.partial(analysis_kernel, steps),
        grid=(steps,),
        in_specs=[
            pl.BlockSpec(memory_space=pltpu.SMEM),
            pl.BlockSpec((1, count), lambda i: (0, 0)),
            pl.BlockSpec((chans // steps, cycles, pixels), lambda i: (i, 0, 0)),
        ],
        out_specs=pl.BlockSpec((count, cycles, 2 * chans), lambda i: (0, 0, 0)),
        out_shape=jax.ShapeDtypeStruct((count, cycles, 2 * chans), BF16),
        scratch_shapes=[
            pltpu.VMEM((pixels, 2 * count), BF16),
            pltpu.VMEM((lane_blocks(2 * count), chans * cycles, 128), F32),
            pltpu.VMEM((lane_blocks(2 * chans), count * cycles, 128), F32),
        ],
        compiler_params=params(),
        name="analysis",
    )(factor, modes.reshape(1, count), sky)


def legendre_kernel(levels, first_ref, degree_ref, band_ref, log_ref, lat_ref, turned_ref, gain_ref, all_ref, pick_ref):
    modes, slots, cycles = lat_ref.shape
    block = 128
    row = lax.broadcasted_iota(jnp.int32, (modes, 1), 0)
    order = jnp.zeros((modes, 1), F32)
    log_seed = jnp.zeros((modes, 1), F32)
    for j in range(modes):
        order = jnp.where(row == j, band_ref[first_ref[0] + j].astype(F32), order)
        log_seed = jnp.where(row == j, log_ref[first_ref[0] + j], log_seed)
    level = lax.broadcasted_iota(jnp.int32, (modes, levels), 1).astype(F32)
    squared = order * order

    def growth(n):
        return jnp.sqrt(jnp.maximum(4.0 * n * n - 1.0, 1.0) / jnp.maximum(n * n - squared, 1.0))

    here = growth(level)
    gain_ref[0] = here
    gain_ref[1] = here / growth(level - 1.0)
    position = (lax.broadcasted_iota(jnp.int32, (1, cycles), 1).astype(F32) + 0.5) / cycles
    colatitude = 0.5 * math.pi + BAND * (2.0 * position - 1.0)
    cosine = jnp.broadcast_to(jnp.cos(colatitude), (modes, cycles))
    orders = jnp.broadcast_to(order, (modes, cycles))
    seed = jnp.exp(log_seed + order * jnp.log(jnp.sin(colatitude)))

    def advance(i, carry):
        latest, earlier = carry
        start = pl.multiple_of(i * block, block)
        first = gain_ref[0, :, pl.ds(start, block)]
        second = gain_ref[1, :, pl.ds(start, block)]
        base = (i * block).astype(F32)
        for n in range(block):
            up = jnp.broadcast_to(first[:, n : n + 1], (modes, cycles)) * cosine
            down = jnp.broadcast_to(second[:, n : n + 1], (modes, cycles))
            begin = jnp.where(orders == base + n, seed, 0.0)
            current = up * latest + (begin - down * earlier)
            put(all_ref, pl.ds(pl.multiple_of((start + n) * modes, modes), modes), current)
            latest, earlier = current, latest
        return latest, earlier

    zero = jnp.zeros((modes, cycles), F32)
    lax.fori_loop(0, levels // block, advance, (zero, zero))

    def pick(s, _):
        source = pl.multiple_of(degree_ref[first_ref[1] + s] * modes, modes)
        for h in range(all_ref.shape[0]):
            pick_ref[h, pl.ds(pl.multiple_of(s * modes, modes), modes), :] = all_ref[h, pl.ds(source, modes), :]
        return 0

    lax.fori_loop(0, slots, pick, 0, unroll=8)
    for j in range(modes):
        rows = get(pick_ref, pl.ds(j, slots, stride=modes), cycles)
        lat_ref[j] = rows.astype(BF16)
        turned_ref[j] = rows.T.astype(BF16)


def legendre(first, degrees, band, modes, slots, cycles):
    levels = degrees.shape[0]
    m = band.astype(F32)
    log_seed = 0.5 * (
        jnp.log(m + 0.5) + lax.lgamma(m + 0.5) - lax.lgamma(m + 1.0) - 0.5 * math.log(math.pi)
    )
    vmem = pl.BlockSpec(memory_space=pltpu.VMEM)
    return pl.pallas_call(
        functools.partial(legendre_kernel, levels),
        in_specs=[pl.BlockSpec(memory_space=pltpu.SMEM)] * 4,
        out_specs=[vmem, vmem],
        out_shape=[
            jax.ShapeDtypeStruct((modes, slots, cycles), BF16),
            jax.ShapeDtypeStruct((modes, cycles, slots), BF16),
        ],
        scratch_shapes=[
            pltpu.VMEM((2, modes, levels), F32),
            pltpu.VMEM((lane_blocks(cycles), levels * modes, 128), F32),
            pltpu.VMEM((lane_blocks(cycles), slots * modes, 128), F32),
        ],
        compiler_params=params(),
        cost_estimate=pl.CostEstimate(flops=40_000_000, bytes_accessed=30_000_000, transcendentals=0),
        name="legendre",
    )(first, degrees, band, log_seed)


def arrange(pieces, low):
    placed = []
    for p in range(len(pieces)):
        value = pieces[p]
        for q in range(1, len(pieces)):
            value = lax.select(low == q, pieces[p ^ q], value)
        placed.append(value)
    return placed


def by_part(placed, chans):
    return [jnp.concatenate([p[:, k * chans : (k + 1) * chans] for p in placed], axis=1) for k in range(2)]


def harmonic_kernel(counts, family, low_ref, lat_ref, *refs):
    spectra, out_ref, turn_ref = refs[: sum(counts)], *refs[sum(counts) :]
    _, modes, cycles, pair = spectra[0].shape
    slots = out_ref.shape[0] * out_ref.shape[1]
    width = out_ref.shape[3]
    for j in range(modes):
        rights = []
        first = 0
        for count in counts:
            pieces = [p[:, j].reshape(p.shape[0] * cycles, pair) for p in spectra[first : first + count]]
            rights.append(pieces[0] if count == 1 else jnp.concatenate(pieces, axis=0))
            first += count
        if family:
            rights = by_part(arrange(rights, low_ref[0]), pair // 2)
        right = rights[0] if len(rights) == 1 else jnp.concatenate(rights, axis=1)
        result = jnp.dot(lat_ref[j], right, preferred_element_type=F32)
        put(turn_ref, pl.ds(j, slots, stride=modes), result)
    out_ref[...] = get(turn_ref, slice(None), width).astype(BF16).reshape(out_ref.shape)


def harmonic(low, lat, spectra, slot_dev, family):
    modes, slots, cycle_total = lat.shape
    _, _, cycles, pair = spectra[0][0].shape
    counts = [len(pieces) for pieces in spectra]
    pieces = sum(spectra, [])
    width = len(spectra) * pair
    dests = slots // slot_dev
    steps = divisor(dests, 2)
    return pl.pallas_call(
        functools.partial(harmonic_kernel, counts, family),
        grid=(steps,),
        in_specs=[
            pl.BlockSpec(memory_space=pltpu.SMEM),
            pl.BlockSpec((modes, slots // steps, cycle_total), lambda i: (0, i, 0)),
        ]
        + [pl.BlockSpec(p.shape, lambda i: (0, 0, 0, 0)) for p in pieces],
        out_specs=pl.BlockSpec((dests // steps, slot_dev, modes, width), lambda i: (i, 0, 0, 0)),
        out_shape=jax.ShapeDtypeStruct((dests, slot_dev, modes, width), BF16),
        scratch_shapes=[pltpu.VMEM((lane_blocks(width), slots // steps * modes, 128), F32)],
        compiler_params=params(),
        cost_estimate=COST,
        name="harmonic",
    )(low, lat, *pieces)


def filter_kernel(counts, wanted, low_ref, filters_ref, *refs):
    inputs, outs, turn_ref = refs[: len(counts)], refs[len(counts) : -1], refs[-1]
    groups, slots, modes, _ = inputs[0].shape
    pair = inputs[0].shape[3] // counts[0]
    chans = pair // 2
    rows = groups * modes
    total = filters_ref.shape[2]
    low, high = low_ref[0], low_ref[1]
    families = total // chans // sum(counts[:2]) if len(counts) > 1 else 1
    width = total // families
    own = pl.multiple_of(high * width, width)
    other = pl.multiple_of((1 - high) * width, width)
    for s in range(slots):
        pieces = []
        for ref, count in zip(inputs[:2], counts):
            pieces += [ref[:, s, :, i * pair : (i + 1) * pair].reshape(rows, pair) for i in range(count)]
        left = jnp.concatenate(by_part(arrange(pieces, low), chans), axis=0)
        if families > 1:
            far = [inputs[2][:, s, :, k * width : (k + 1) * width].reshape(rows, width) for k in range(2)]
            left = jnp.concatenate([left, jnp.concatenate(far, axis=0)], axis=1)
        lane = 0
        for family, hops in wanted:
            if family:
                start, count = other, width
            else:
                start, count = pl.multiple_of(own + (low ^ hops) * chans, chans), chans
            right = filters_ref[s, pl.ds(start, count), pl.ds(own, width)]
            if families > 1:
                right = jnp.concatenate([right, filters_ref[s, pl.ds(start, count), pl.ds(other, width)]], axis=1)
            result = lax.dot_general(left, right, (((1,), (1,)), ((), ())), preferred_element_type=F32)
            result = jnp.concatenate([result[:rows], result[rows:]], axis=1)
            blocks = lane_blocks(2 * count)
            put(turn_ref.at[lane : lane + blocks], pl.ds(s, rows, stride=slots), result)
            lane += blocks
    lane = 0
    for (family, hops), ref in zip(wanted, outs):
        blocks = lane_blocks(ref.shape[3])
        value = get(turn_ref.at[lane : lane + blocks], slice(None), ref.shape[3])
        ref[...] = value.astype(BF16).reshape(ref.shape)
        lane += blocks


def apply_filters(place, filters, coeffs, counts, wanted):
    groups, slots, modes, _ = coeffs[0].shape
    total = filters.shape[2]
    pair = coeffs[0].shape[3] // counts[0]
    step = min(slots, 16)
    widths = [counts[-1] * pair if family else pair for family, _ in wanted]
    return pl.pallas_call(
        functools.partial(filter_kernel, counts, wanted),
        grid=(slots // step,),
        in_specs=[
            pl.BlockSpec(memory_space=pltpu.SMEM),
            pl.BlockSpec((step, total, total), lambda i: (i, 0, 0)),
        ]
        + [pl.BlockSpec((groups, step, modes, c.shape[3]), lambda i: (0, i, 0, 0)) for c in coeffs],
        out_specs=[pl.BlockSpec((groups, modes, step, w), lambda i: (0, 0, i, 0)) for w in widths],
        out_shape=[jax.ShapeDtypeStruct((groups, modes, slots, w), BF16) for w in widths],
        scratch_shapes=[pltpu.VMEM((sum(lane_blocks(w) for w in widths), groups * modes * step, 128), F32)],
        compiler_params=params(),
        cost_estimate=COST,
        name="filters",
    )(place, filters, *coeffs)


def cycles_kernel(scale, low_ref, turned_ref, filtered_ref, *outs):
    groups, modes, slot_dev, width = filtered_ref.shape
    blocks, _, cycles, pair = outs[0].shape
    chans = pair // 2
    parts = len(outs)
    for j in range(modes):
        result = jnp.dot(
            turned_ref[j],
            filtered_ref[:, j].reshape(groups * slot_dev, width),
            preferred_element_type=F32,
        )
        result = result * scale
        if parts == 1:
            pieces = [result]
        else:
            half = width // 2
            pieces = [
                jnp.concatenate([result[:, k * half + p * chans : k * half + (p + 1) * chans] for k in range(2)], axis=1)
                for p in range(parts)
            ]
            pieces = arrange(pieces, low_ref[0])
        for piece, ref in zip(pieces, outs):
            ref[:, j] = piece.astype(BF16).reshape(blocks, cycles, pair)


def to_cycles(low, turned, filtered, scale, blocks, parts):
    modes, cycle_total, slots = turned.shape
    width = filtered.shape[3]
    vmem = pl.BlockSpec(memory_space=pltpu.VMEM)
    shape = (blocks, modes, cycle_total // blocks, width // parts)
    return pl.pallas_call(
        functools.partial(cycles_kernel, scale),
        in_specs=[pl.BlockSpec(memory_space=pltpu.SMEM), vmem, vmem],
        out_specs=[vmem] * parts,
        out_shape=[jax.ShapeDtypeStruct(shape, BF16)] * parts,
        compiler_params=params(),
        cost_estimate=COST,
        name="cycles",
    )(low, turned, filtered)


def phases_kernel(modes_ref, phase_ref):
    modes, pixels = modes_ref.shape[0], phase_ref.shape[1]
    low = 128
    ids = modes_ref[...]
    unit = 2.0 * math.pi / pixels

    def table(columns, stride):
        index = lax.broadcasted_iota(jnp.int32, (modes, columns), 1) * stride
        angle = unit * ((index * ids) & (pixels - 1)).astype(F32)
        return jnp.cos(angle), jnp.sin(angle)

    cos_low, sin_low = table(low, 1)
    cos_high, sin_high = table(pixels // low, low)
    for h in range(pixels // low):
        ca, sa = cos_high[:, h : h + 1], sin_high[:, h : h + 1]
        columns = slice(h * low, (h + 1) * low)
        phase_ref[:modes, columns] = (ca * cos_low - sa * sin_low).astype(BF16)
        phase_ref[modes:, columns] = (-(sa * cos_low + ca * sin_low)).astype(BF16)


def phases_of(modes, pixels):
    count = modes.shape[0]
    vmem = pl.BlockSpec(memory_space=pltpu.VMEM)
    return pl.pallas_call(
        phases_kernel,
        in_specs=[vmem],
        out_specs=vmem,
        out_shape=jax.ShapeDtypeStruct((2 * count, pixels), BF16),
        compiler_params=params(),
        cost_estimate=COST,
        name="phases",
    )(modes.reshape(count, 1))


def synthesis_kernel(phase_ref, parts_ref, out_ref, there_ref, wide_ref, turn_ref, left_ref, sent):
    chans, cycles, pixels = there_ref.shape
    steps = sent.shape[0]
    modes, _, pair = parts_ref.shape
    total = pair // 2
    put(wide_ref, slice(None), parts_ref[...].astype(F32).reshape(modes * cycles, pair))
    for r in range(cycles):
        part = get(wide_ref, pl.ds(r, modes, stride=cycles), pair)
        both = [part[:, k * total : (k + 1) * total].T for k in range(2)]
        put(turn_ref, pl.ds(r, total, stride=cycles), jnp.concatenate(both, axis=1))
    left_ref[...] = get(turn_ref, slice(None), 2 * modes).astype(BF16)

    part = chans // steps
    rows = part * cycles
    copies = []
    for i in range(steps):
        left = left_ref[i * rows : (i + 1) * rows, :]
        result = jnp.dot(left, phase_ref[...], preferred_element_type=F32) * (1.0 / math.sqrt(modes))
        there_ref[i * part : (i + 1) * part] = result.astype(BF16).reshape(part, cycles, pixels)
        window = pl.ds(i * part, part)
        copies.append(pltpu.make_async_copy(there_ref.at[window], out_ref.at[window], sent.at[i]))
        copies[i].start()
    for copy in copies:
        copy.wait()


def synthesis(parts, phases):
    count, cycles, pair = parts.shape
    pixels = phases.shape[1]
    chans = pair // 2
    steps = divisor(chans, 8)
    vmem = pl.BlockSpec(memory_space=pltpu.VMEM)
    return pl.pallas_call(
        synthesis_kernel,
        in_specs=[vmem, vmem],
        out_specs=pl.BlockSpec(memory_space=pl.ANY),
        out_shape=jax.ShapeDtypeStruct((chans, cycles, pixels), BF16),
        scratch_shapes=[
            pltpu.VMEM((chans, cycles, pixels), BF16),
            pltpu.VMEM((lane_blocks(pair), count * cycles, 128), F32),
            pltpu.VMEM((lane_blocks(2 * count), chans * cycles, 128), F32),
            pltpu.VMEM((chans * cycles, 2 * count), BF16),
            pltpu.SemaphoreType.DMA((steps,)),
        ],
        compiler_params=params(),
        name="synthesis",
    )(phases, parts)


def body(sky_maps, filters, band_order_values, slot_degree_values):
    chans, cycle_dev, pixels = sky_maps.shape
    chan_groups = lax.axis_size("chan")
    blk_groups = lax.axis_size("blk")
    chan, blk = lax.axis_index("chan"), lax.axis_index("blk")
    slot_dev = filters.shape[0]
    degree_count = slot_degree_values.shape[0]
    mode_dev = band_order_values.shape[0] // blk_groups
    cycle_total = cycle_dev * blk_groups
    group_slots = slot_dev * blk_groups
    colatitude = polar_angle_values(cycle_total)
    cycle_factor = (
        2.0 * math.sqrt(2.0 * BAND / cycle_total) * jnp.sin(colatitude) * (1.0 / math.sqrt(pixels))
    )
    local_factor = lax.dynamic_slice_in_dim(cycle_factor, blk * cycle_dev, cycle_dev)
    spectra = analysis(sky_maps, local_factor, band_order_values)
    spectra = spectra.reshape(blk_groups, mode_dev, cycle_dev, 2 * chans)
    def swap(value, t):
        return lax.ppermute(value, "chan", [(i, i ^ t) for i in range(chan_groups)])

    def exchange(value):
        return lax.all_to_all(value, "blk", split_axis=0, concat_axis=0, tiled=True)

    near = max(1, chan_groups // 2)
    hops = [[0], list(range(1, near)), list(range(near, chan_groups))]
    hops = [h for h in hops if h]
    counts = [len(h) for h in hops]
    place = jnp.stack([chan % near, chan // near])
    first = jnp.stack([blk * mode_dev, chan * group_slots])
    lat, turned = legendre(first, slot_degree_values, band_order_values, mode_dev, group_slots, cycle_total)
    own = exchange(spectra)
    gathered = [[own]]
    half = max(1, blk_groups * 4 // 8)
    if chan_groups > 1:
        beside = swap(spectra, 1)
        beside, lat, own = lax.optimization_barrier((beside, lat, own))
        beside = exchange(beside)
        gathered = [[own], [beside]]
    for t in range(2, chan_groups):
        top = 1 << (t.bit_length() - 1)
        source = [own[:half], own[half:]] if t == top else gathered[top]
        gathered.append([swap(piece, t if t == top else t ^ top) for piece in source])
    coeffs = []
    for n, part in enumerate(hops):
        result = harmonic(place, lat, [gathered[t] for t in part], slot_dev, n == 2)
        if n == 0 and chan_groups > 1:
            result, gathered[1][0] = lax.optimization_barrier((result, gathered[1][0]))
            if chan_groups > 2:
                result, gathered[2][0] = lax.optimization_barrier((result, gathered[2][0]))
        if n == 1:
            result, coeffs[0] = lax.optimization_barrier((result, coeffs[0]))
            if chan_groups > 2:
                result, gathered[2][1], gathered[3][0] = lax.optimization_barrier((result, gathered[2][1], gathered[3][0]))
        if n == 2:
            result, coeffs[1] = lax.optimization_barrier((result, coeffs[1]))
        lat, result = lax.optimization_barrier((lat, result))
        coeffs.append(exchange(result))
    scale = 2.0 / math.sqrt(degree_count)
    partial = {}
    tasks = [[(False, t)] for part in hops[:2] for t in part][::-1]
    if len(hops) == 3:
        tasks = [[(True, None)]] + [sum(tasks, [])]
    else:
        tasks = [sum(tasks, [])]
    for n, task in enumerate(tasks):
        results = list(apply_filters(place, filters, coeffs, counts, task))
        place, results[0] = lax.optimization_barrier((place, results[0]))
        for (family, t), filtered in zip(task, results):
            names = hops[2] if family else [t]
            outs = to_cycles(place, turned, exchange(filtered), scale, blk_groups, len(names))
            partial.update(zip(names, outs))
    total = partial[0].astype(F32)
    top = chan_groups // 2
    while top:
        group = partial[top].astype(F32)
        for t in range(top + 1, 2 * top):
            group = group + swap(partial[t], t ^ top).astype(F32)
        total = total + swap(group.astype(BF16), top).astype(F32)
        top //= 2
    cycle_part = total.astype(BF16)
    by_cycle = lax.all_to_all(cycle_part, "blk", split_axis=0, concat_axis=0, tiled=True)
    by_cycle = by_cycle.reshape(blk_groups * mode_dev, cycle_dev, 2 * chans)
    return synthesis(by_cycle, phases_of(band_order_values, pixels))


def solution(mesh):
    in_specs = (P("chan", "blk", None), P(("chan", "blk"), None, None), P(), P())
    out_specs = P("chan", "blk", None)
    return jax.shard_map(body, mesh=mesh, in_specs=in_specs, out_specs=out_specs, check_vma=False)
```

```python
import functools
import math

import jax
import jax.numpy as jnp
from jax import lax
from jax.experimental import pallas as pl
from jax.experimental.pallas import tpu as pltpu
from jax.sharding import PartitionSpec as P

BAND = 0.38
VMEM_LIMIT = 52 * 1024 * 1024
F32 = jnp.float32
BF16 = jnp.bfloat16
COST = pl.CostEstimate(flops=2_000_000_000, bytes_accessed=12_000_000, transcendentals=0)


def params(**kw):
    return pltpu.CompilerParams(vmem_limit_bytes=VMEM_LIMIT, **kw)


def polar_angle_values(cycle_total):
    position = (jnp.arange(cycle_total, dtype=F32) + 0.5) / cycle_total
    return 0.5 * math.pi + BAND * (2.0 * position - 1.0)


def divisor(n, most):
    return max(d for d in range(1, most + 1) if n % d == 0)


def lane_blocks(width):
    return -(-width // 128)


def put(ref, rows, value):
    width = value.shape[1]
    for h in range(ref.shape[0]):
        piece = value[:, h * 128 : min((h + 1) * 128, width)]
        if piece.shape[1] < 128:
            piece = jnp.concatenate([piece, jnp.zeros((piece.shape[0], 128 - piece.shape[1]), piece.dtype)], axis=1)
        ref[h, rows, :] = piece


def get(ref, rows, width):
    value = jnp.concatenate([ref[h, rows, :] for h in range(ref.shape[0])], axis=1)
    return value if width == value.shape[1] else value[:, :width]


def analysis_kernel(steps, factor_ref, modes_ref, sky_ref, out_ref, phase_ref, prod_ref, turn_ref):
    step = pl.program_id(0)
    chans, cycles, pixels = sky_ref.shape
    modes = modes_ref.shape[1]
    low = 64
    high = pixels // low

    @pl.when(step == 0)
    def _():
        ids = modes_ref[...]
        unit = 2.0 * math.pi / pixels

        def table(rows, stride):
            index = lax.broadcasted_iota(jnp.int32, (rows, modes), 0) * stride
            angle = unit * ((index * ids) & (pixels - 1)).astype(F32)
            return jnp.cos(angle), jnp.sin(angle)

        cos_low, sin_low = table(low, 1)
        cos_high, sin_high = table(high, low)
        for h in range(high):
            ca, sa = cos_high[h : h + 1], sin_high[h : h + 1]
            rows = slice(h * low, (h + 1) * low)
            phase_ref[rows, :modes] = (ca * cos_low - sa * sin_low).astype(BF16)
            phase_ref[rows, modes:] = (-(sa * cos_low + ca * sin_low)).astype(BF16)

    rows = chans * cycles
    product = jnp.dot(sky_ref[...].reshape(rows, pixels), phase_ref[...], preferred_element_type=F32)
    put(prod_ref, pl.ds(pl.multiple_of(step * rows, rows), rows), product)

    @pl.when(step == steps - 1)
    def _():
        total = chans * steps
        for r in range(cycles):
            part = get(prod_ref, pl.ds(r, total, stride=cycles), 2 * modes) * factor_ref[r]
            both = [part[:, k * modes : (k + 1) * modes].T for k in range(2)]
            put(turn_ref, pl.ds(r, modes, stride=cycles), jnp.concatenate(both, axis=1))
        out_ref[...] = get(turn_ref, slice(None), 2 * total).astype(BF16).reshape(out_ref.shape)


def analysis(sky, factor, modes):
    chans, cycles, pixels = sky.shape
    count = modes.shape[0]
    steps = divisor(chans, 2)
    return pl.pallas_call(
        functools.partial(analysis_kernel, steps),
        grid=(steps,),
        in_specs=[
            pl.BlockSpec(memory_space=pltpu.SMEM),
            pl.BlockSpec((1, count), lambda i: (0, 0)),
            pl.BlockSpec((chans // steps, cycles, pixels), lambda i: (i, 0, 0)),
        ],
        out_specs=pl.BlockSpec((count, cycles, 2 * chans), lambda i: (0, 0, 0)),
        out_shape=jax.ShapeDtypeStruct((count, cycles, 2 * chans), BF16),
        scratch_shapes=[
            pltpu.VMEM((pixels, 2 * count), BF16),
            pltpu.VMEM((lane_blocks(2 * count), chans * cycles, 128), F32),
            pltpu.VMEM((lane_blocks(2 * chans), count * cycles, 128), F32),
        ],
        compiler_params=params(),
        name="analysis",
    )(factor, modes.reshape(1, count), sky)


def legendre_kernel(levels, first_ref, degree_ref, band_ref, log_ref, lat_ref, turned_ref, gain_ref, all_ref, pick_ref):
    modes, slots, cycles = lat_ref.shape
    block = 128
    row = lax.broadcasted_iota(jnp.int32, (modes, 1), 0)
    order = jnp.zeros((modes, 1), F32)
    log_seed = jnp.zeros((modes, 1), F32)
    for j in range(modes):
        order = jnp.where(row == j, band_ref[first_ref[0] + j].astype(F32), order)
        log_seed = jnp.where(row == j, log_ref[first_ref[0] + j], log_seed)
    level = lax.broadcasted_iota(jnp.int32, (modes, levels), 1).astype(F32)
    squared = order * order

    def growth(n):
        return jnp.sqrt(jnp.maximum(4.0 * n * n - 1.0, 1.0) / jnp.maximum(n * n - squared, 1.0))

    here = growth(level)
    gain_ref[0] = here
    gain_ref[1] = here / growth(level - 1.0)
    position = (lax.broadcasted_iota(jnp.int32, (1, cycles), 1).astype(F32) + 0.5) / cycles
    colatitude = 0.5 * math.pi + BAND * (2.0 * position - 1.0)
    cosine = jnp.broadcast_to(jnp.cos(colatitude), (modes, cycles))
    orders = jnp.broadcast_to(order, (modes, cycles))
    seed = jnp.exp(log_seed + order * jnp.log(jnp.sin(colatitude)))

    def advance(i, carry):
        latest, earlier = carry
        start = pl.multiple_of(i * block, block)
        first = gain_ref[0, :, pl.ds(start, block)]
        second = gain_ref[1, :, pl.ds(start, block)]
        base = (i * block).astype(F32)
        for n in range(block):
            up = jnp.broadcast_to(first[:, n : n + 1], (modes, cycles)) * cosine
            down = jnp.broadcast_to(second[:, n : n + 1], (modes, cycles))
            begin = jnp.where(orders == base + n, seed, 0.0)
            current = up * latest + (begin - down * earlier)
            put(all_ref, pl.ds(pl.multiple_of((start + n) * modes, modes), modes), current)
            latest, earlier = current, latest
        return latest, earlier

    zero = jnp.zeros((modes, cycles), F32)
    lax.fori_loop(0, levels // block, advance, (zero, zero))

    def pick(s, _):
        source = pl.multiple_of(degree_ref[first_ref[1] + s] * modes, modes)
        for h in range(all_ref.shape[0]):
            pick_ref[h, pl.ds(pl.multiple_of(s * modes, modes), modes), :] = all_ref[h, pl.ds(source, modes), :]
        return 0

    lax.fori_loop(0, slots, pick, 0, unroll=8)
    for j in range(modes):
        rows = get(pick_ref, pl.ds(j, slots, stride=modes), cycles)
        lat_ref[j] = rows.astype(BF16)
        turned_ref[j] = rows.T.astype(BF16)


def legendre(first, degrees, band, modes, slots, cycles):
    levels = degrees.shape[0]
    m = band.astype(F32)
    log_seed = 0.5 * (
        jnp.log(m + 0.5) + lax.lgamma(m + 0.5) - lax.lgamma(m + 1.0) - 0.5 * math.log(math.pi)
    )
    vmem = pl.BlockSpec(memory_space=pltpu.VMEM)
    return pl.pallas_call(
        functools.partial(legendre_kernel, levels),
        in_specs=[pl.BlockSpec(memory_space=pltpu.SMEM)] * 4,
        out_specs=[vmem, vmem],
        out_shape=[
            jax.ShapeDtypeStruct((modes, slots, cycles), BF16),
            jax.ShapeDtypeStruct((modes, cycles, slots), BF16),
        ],
        scratch_shapes=[
            pltpu.VMEM((2, modes, levels), F32),
            pltpu.VMEM((lane_blocks(cycles), levels * modes, 128), F32),
            pltpu.VMEM((lane_blocks(cycles), slots * modes, 128), F32),
        ],
        compiler_params=params(),
        cost_estimate=pl.CostEstimate(flops=40_000_000, bytes_accessed=30_000_000, transcendentals=0),
        name="legendre",
    )(first, degrees, band, log_seed)


def arrange(pieces, low):
    placed = []
    for p in range(len(pieces)):
        value = pieces[p]
        for q in range(1, len(pieces)):
            value = lax.select(low == q, pieces[p ^ q], value)
        placed.append(value)
    return placed


def by_part(placed, chans):
    return [jnp.concatenate([p[:, k * chans : (k + 1) * chans] for p in placed], axis=1) for k in range(2)]


def harmonic_kernel(counts, family, low_ref, lat_ref, *refs):
    spectra, out_ref, turn_ref = refs[: sum(counts)], *refs[sum(counts) :]
    _, modes, cycles, pair = spectra[0].shape
    slots = out_ref.shape[0] * out_ref.shape[1]
    width = out_ref.shape[3]
    for j in range(modes):
        rights = []
        first = 0
        for count in counts:
            pieces = [p[:, j].reshape(p.shape[0] * cycles, pair) for p in spectra[first : first + count]]
            rights.append(pieces[0] if count == 1 else jnp.concatenate(pieces, axis=0))
            first += count
        if family:
            rights = by_part(arrange(rights, low_ref[0]), pair // 2)
        right = rights[0] if len(rights) == 1 else jnp.concatenate(rights, axis=1)
        result = jnp.dot(lat_ref[j], right, preferred_element_type=F32)
        put(turn_ref, pl.ds(j, slots, stride=modes), result)
    out_ref[...] = get(turn_ref, slice(None), width).astype(BF16).reshape(out_ref.shape)


def harmonic(low, lat, spectra, slot_dev, family):
    modes, slots, cycle_total = lat.shape
    _, _, cycles, pair = spectra[0][0].shape
    counts = [len(pieces) for pieces in spectra]
    pieces = sum(spectra, [])
    width = len(spectra) * pair
    dests = slots // slot_dev
    steps = divisor(dests, 2)
    return pl.pallas_call(
        functools.partial(harmonic_kernel, counts, family),
        grid=(steps,),
        in_specs=[
            pl.BlockSpec(memory_space=pltpu.SMEM),
            pl.BlockSpec((modes, slots // steps, cycle_total), lambda i: (0, i, 0)),
        ]
        + [pl.BlockSpec(p.shape, lambda i: (0, 0, 0, 0)) for p in pieces],
        out_specs=pl.BlockSpec((dests // steps, slot_dev, modes, width), lambda i: (i, 0, 0, 0)),
        out_shape=jax.ShapeDtypeStruct((dests, slot_dev, modes, width), BF16),
        scratch_shapes=[pltpu.VMEM((lane_blocks(width), slots // steps * modes, 128), F32)],
        compiler_params=params(),
        cost_estimate=COST,
        name="harmonic",
    )(low, lat, *pieces)


def filter_kernel(counts, wanted, low_ref, filters_ref, *refs):
    inputs, outs, turn_ref = refs[: len(counts)], refs[len(counts) : -1], refs[-1]
    groups, slots, modes, _ = inputs[0].shape
    pair = inputs[0].shape[3] // counts[0]
    chans = pair // 2
    rows = groups * modes
    total = filters_ref.shape[2]
    low, high = low_ref[0], low_ref[1]
    families = total // chans // sum(counts[:2]) if len(counts) > 1 else 1
    width = total // families
    own = pl.multiple_of(high * width, width)
    other = pl.multiple_of((1 - high) * width, width)
    for s in range(slots):
        pieces = []
        for ref, count in zip(inputs[:2], counts):
            pieces += [ref[:, s, :, i * pair : (i + 1) * pair].reshape(rows, pair) for i in range(count)]
        left = jnp.concatenate(by_part(arrange(pieces, low), chans), axis=0)
        if families > 1:
            far = [inputs[2][:, s, :, k * width : (k + 1) * width].reshape(rows, width) for k in range(2)]
            left = jnp.concatenate([left, jnp.concatenate(far, axis=0)], axis=1)
        lane = 0
        for family, hops in wanted:
            if family:
                start, count = other, width
            else:
                start, count = pl.multiple_of(own + (low ^ hops) * chans, chans), chans
            right = filters_ref[s, pl.ds(start, count), pl.ds(own, width)]
            if families > 1:
                right = jnp.concatenate([right, filters_ref[s, pl.ds(start, count), pl.ds(other, width)]], axis=1)
            result = lax.dot_general(left, right, (((1,), (1,)), ((), ())), preferred_element_type=F32)
            result = jnp.concatenate([result[:rows], result[rows:]], axis=1)
            blocks = lane_blocks(2 * count)
            put(turn_ref.at[lane : lane + blocks], pl.ds(s, rows, stride=slots), result)
            lane += blocks
    lane = 0
    for (family, hops), ref in zip(wanted, outs):
        blocks = lane_blocks(ref.shape[3])
        value = get(turn_ref.at[lane : lane + blocks], slice(None), ref.shape[3])
        ref[...] = value.astype(BF16).reshape(ref.shape)
        lane += blocks


def apply_filters(place, filters, coeffs, counts, wanted):
    groups, slots, modes, _ = coeffs[0].shape
    total = filters.shape[2]
    pair = coeffs[0].shape[3] // counts[0]
    step = min(slots, 16)
    widths = [counts[-1] * pair if family else pair for family, _ in wanted]
    return pl.pallas_call(
        functools.partial(filter_kernel, counts, wanted),
        grid=(slots // step,),
        in_specs=[
            pl.BlockSpec(memory_space=pltpu.SMEM),
            pl.BlockSpec((step, total, total), lambda i: (i, 0, 0)),
        ]
        + [pl.BlockSpec((groups, step, modes, c.shape[3]), lambda i: (0, i, 0, 0)) for c in coeffs],
        out_specs=[pl.BlockSpec((groups, modes, step, w), lambda i: (0, 0, i, 0)) for w in widths],
        out_shape=[jax.ShapeDtypeStruct((groups, modes, slots, w), BF16) for w in widths],
        scratch_shapes=[pltpu.VMEM((sum(lane_blocks(w) for w in widths), groups * modes * step, 128), F32)],
        compiler_params=params(),
        cost_estimate=COST,
        name="filters",
    )(place, filters, *coeffs)


def cycles_kernel(scale, low_ref, turned_ref, filtered_ref, *outs):
    groups, modes, slot_dev, width = filtered_ref.shape
    blocks, _, cycles, pair = outs[0].shape
    chans = pair // 2
    parts = len(outs)
    for j in range(modes):
        result = jnp.dot(
            turned_ref[j],
            filtered_ref[:, j].reshape(groups * slot_dev, width),
            preferred_element_type=F32,
        )
        result = result * scale
        if parts == 1:
            pieces = [result]
        else:
            half = width // 2
            pieces = [
                jnp.concatenate([result[:, k * half + p * chans : k * half + (p + 1) * chans] for k in range(2)], axis=1)
                for p in range(parts)
            ]
            pieces = arrange(pieces, low_ref[0])
        for piece, ref in zip(pieces, outs):
            ref[:, j] = piece.astype(BF16).reshape(blocks, cycles, pair)


def to_cycles(low, turned, filtered, scale, blocks, parts):
    modes, cycle_total, slots = turned.shape
    width = filtered.shape[3]
    groups, slot_dev = filtered.shape[0], filtered.shape[2]
    steps = divisor(modes, 2)
    shape = (blocks, modes, cycle_total // blocks, width // parts)
    return pl.pallas_call(
        functools.partial(cycles_kernel, scale),
        grid=(steps,),
        in_specs=[
            pl.BlockSpec(memory_space=pltpu.SMEM),
            pl.BlockSpec((modes // steps, cycle_total, slots), lambda i: (i, 0, 0)),
            pl.BlockSpec((groups, modes // steps, slot_dev, width), lambda i: (0, i, 0, 0)),
        ],
        out_specs=[pl.BlockSpec((blocks, modes // steps) + shape[2:], lambda i: (0, i, 0, 0))] * parts,
        out_shape=[jax.ShapeDtypeStruct(shape, BF16)] * parts,
        compiler_params=params(),
        cost_estimate=COST,
        name="cycles",
    )(low, turned, filtered)


def phases_kernel(modes_ref, phase_ref):
    modes, pixels = modes_ref.shape[0], phase_ref.shape[1]
    low = 128
    ids = modes_ref[...]
    unit = 2.0 * math.pi / pixels

    def table(columns, stride):
        index = lax.broadcasted_iota(jnp.int32, (modes, columns), 1) * stride
        angle = unit * ((index * ids) & (pixels - 1)).astype(F32)
        return jnp.cos(angle), jnp.sin(angle)

    cos_low, sin_low = table(low, 1)
    cos_high, sin_high = table(pixels // low, low)
    for h in range(pixels // low):
        ca, sa = cos_high[:, h : h + 1], sin_high[:, h : h + 1]
        columns = slice(h * low, (h + 1) * low)
        phase_ref[:modes, columns] = (ca * cos_low - sa * sin_low).astype(BF16)
        phase_ref[modes:, columns] = (-(sa * cos_low + ca * sin_low)).astype(BF16)


def phases_of(modes, pixels):
    count = modes.shape[0]
    vmem = pl.BlockSpec(memory_space=pltpu.VMEM)
    return pl.pallas_call(
        phases_kernel,
        in_specs=[vmem],
        out_specs=vmem,
        out_shape=jax.ShapeDtypeStruct((2 * count, pixels), BF16),
        compiler_params=params(),
        cost_estimate=COST,
        name="phases",
    )(modes.reshape(count, 1))


def synthesis_kernel(phase_ref, parts_ref, out_ref, there_ref, wide_ref, turn_ref, left_ref, sent):
    chans, cycles, pixels = there_ref.shape
    steps = sent.shape[0]
    modes, _, pair = parts_ref.shape
    total = pair // 2
    put(wide_ref, slice(None), parts_ref[...].astype(F32).reshape(modes * cycles, pair))
    for r in range(cycles):
        part = get(wide_ref, pl.ds(r, modes, stride=cycles), pair)
        both = [part[:, k * total : (k + 1) * total].T for k in range(2)]
        put(turn_ref, pl.ds(r, total, stride=cycles), jnp.concatenate(both, axis=1))
    left_ref[...] = get(turn_ref, slice(None), 2 * modes).astype(BF16)

    part = chans // steps
    rows = part * cycles
    copies = []
    for i in range(steps):
        left = left_ref[i * rows : (i + 1) * rows, :]
        result = jnp.dot(left, phase_ref[...], preferred_element_type=F32) * (1.0 / math.sqrt(modes))
        there_ref[i * part : (i + 1) * part] = result.astype(BF16).reshape(part, cycles, pixels)
        window = pl.ds(i * part, part)
        copies.append(pltpu.make_async_copy(there_ref.at[window], out_ref.at[window], sent.at[i]))
        copies[i].start()
    for copy in copies:
        copy.wait()


def synthesis(parts, phases):
    count, cycles, pair = parts.shape
    pixels = phases.shape[1]
    chans = pair // 2
    steps = divisor(chans, 8)
    vmem = pl.BlockSpec(memory_space=pltpu.VMEM)
    return pl.pallas_call(
        synthesis_kernel,
        in_specs=[vmem, vmem],
        out_specs=pl.BlockSpec(memory_space=pl.ANY),
        out_shape=jax.ShapeDtypeStruct((chans, cycles, pixels), BF16),
        scratch_shapes=[
            pltpu.VMEM((chans, cycles, pixels), BF16),
            pltpu.VMEM((lane_blocks(pair), count * cycles, 128), F32),
            pltpu.VMEM((lane_blocks(2 * count), chans * cycles, 128), F32),
            pltpu.VMEM((chans * cycles, 2 * count), BF16),
            pltpu.SemaphoreType.DMA((steps,)),
        ],
        compiler_params=params(),
        name="synthesis",
    )(phases, parts)


def body(sky_maps, filters, band_order_values, slot_degree_values):
    chans, cycle_dev, pixels = sky_maps.shape
    chan_groups = lax.axis_size("chan")
    blk_groups = lax.axis_size("blk")
    chan, blk = lax.axis_index("chan"), lax.axis_index("blk")
    slot_dev = filters.shape[0]
    degree_count = slot_degree_values.shape[0]
    mode_dev = band_order_values.shape[0] // blk_groups
    cycle_total = cycle_dev * blk_groups
    group_slots = slot_dev * blk_groups
    colatitude = polar_angle_values(cycle_total)
    cycle_factor = (
        2.0 * math.sqrt(2.0 * BAND / cycle_total) * jnp.sin(colatitude) * (1.0 / math.sqrt(pixels))
    )
    local_factor = lax.dynamic_slice_in_dim(cycle_factor, blk * cycle_dev, cycle_dev)
    spectra = analysis(sky_maps, local_factor, band_order_values)
    spectra = spectra.reshape(blk_groups, mode_dev, cycle_dev, 2 * chans)
    def swap(value, t):
        return lax.ppermute(value, "chan", [(i, i ^ t) for i in range(chan_groups)])

    def exchange(value):
        return lax.all_to_all(value, "blk", split_axis=0, concat_axis=0, tiled=True)

    near = max(1, chan_groups // 2)
    hops = [[0], list(range(1, near)), list(range(near, chan_groups))]
    hops = [h for h in hops if h]
    counts = [len(h) for h in hops]
    place = jnp.stack([chan % near, chan // near])
    first = jnp.stack([blk * mode_dev, chan * group_slots])
    lat, turned = legendre(first, slot_degree_values, band_order_values, mode_dev, group_slots, cycle_total)
    own = exchange(spectra)
    gathered = [[own]]
    half = max(1, blk_groups * 4 // 8)
    if chan_groups > 1:
        beside = swap(spectra, 1)
        beside, lat, own = lax.optimization_barrier((beside, lat, own))
        beside = exchange(beside)
        gathered = [[own], [beside]]
    for t in range(2, chan_groups):
        top = 1 << (t.bit_length() - 1)
        source = [own[:half], own[half:]] if t == top else gathered[top]
        gathered.append([swap(piece, t if t == top else t ^ top) for piece in source])
    coeffs = []
    for n, part in enumerate(hops):
        result = harmonic(place, lat, [gathered[t] for t in part], slot_dev, n == 2)
        if n == 0 and chan_groups > 1:
            result, gathered[1][0] = lax.optimization_barrier((result, gathered[1][0]))
            if chan_groups > 2:
                result, gathered[2][0] = lax.optimization_barrier((result, gathered[2][0]))
        if n == 1:
            result, coeffs[0] = lax.optimization_barrier((result, coeffs[0]))
            if chan_groups > 2:
                result, gathered[2][1], gathered[3][0] = lax.optimization_barrier((result, gathered[2][1], gathered[3][0]))
        if n == 2:
            result, coeffs[1] = lax.optimization_barrier((result, coeffs[1]))
        lat, result = lax.optimization_barrier((lat, result))
        coeffs.append(exchange(result))
    scale = 2.0 / math.sqrt(degree_count)
    partial = {}
    tasks = [[(False, t)] for part in hops[:2] for t in part][::-1]
    if len(hops) == 3:
        tasks = [[(True, None)]] + [sum(tasks, [])]
    else:
        tasks = [sum(tasks, [])]
    for n, task in enumerate(tasks):
        results = list(apply_filters(place, filters, coeffs, counts, task))
        place, results[0] = lax.optimization_barrier((place, results[0]))
        for (family, t), filtered in zip(task, results):
            names = hops[2] if family else [t]
            outs = to_cycles(place, turned, exchange(filtered), scale, blk_groups, len(names))
            partial.update(zip(names, outs))
    total = partial[0].astype(F32)
    top = chan_groups // 2
    while top:
        group = partial[top].astype(F32)
        for t in range(top + 1, 2 * top):
            group = group + swap(partial[t], t ^ top).astype(F32)
        total = total + swap(group.astype(BF16), top).astype(F32)
        top //= 2
    cycle_part = total.astype(BF16)
    by_cycle = lax.all_to_all(cycle_part, "blk", split_axis=0, concat_axis=0, tiled=True)
    by_cycle = by_cycle.reshape(blk_groups * mode_dev, cycle_dev, 2 * chans)
    return synthesis(by_cycle, phases_of(band_order_values, pixels))


def solution(mesh):
    in_specs = (P("chan", "blk", None), P(("chan", "blk"), None, None), P(), P())
    out_specs = P("chan", "blk", None)
    return jax.shard_map(body, mesh=mesh, in_specs=in_specs, out_specs=out_specs, check_vma=False)
```
